128 devices in a mesh: param: 32 (over z, y, core), ex: 4 (over x).
Axes of the slice: x: 4, y: 4, z: 4, core: 2. Of those that a mesh axis runs over, the one named last changes fastest.
Arguments:
- inputs: bfloat16 [16, 128, 4096], P('ex', None, 'param'), may hold values from -6 to 6
- cotangents: bfloat16 [3, 16, 128, 4096], P(None, 'ex', None, 'param'), may hold values from -6 to 6
- jl_bank: bfloat16 [64, 128, 128], replicated, may hold values from -0.5 to 0.5
- jl_tiles: int32 [3, 32, 32, 8], replicated, may hold values from 0 to 63
- jl_blocks: int32 [3, 32, 32, 8], replicated, may hold values from 0 to 31
- jl_signs: int32 [3, 32, 32, 8], replicated, may hold values from 0 to 1
- test_features: bfloat16 [1024, 4096], P('ex', 'param'), may hold values from -6 to 6
Outputs:
- scores: float32 [16, 1024], P('ex')
The draws below stay inside these ranges and needn't reach their ends.
All inputs are finite; a program needn't handle non-finite values.
Results may differ from the reference program's by a relative error of at most 0.007.
Values may be sent and summed in bfloat16 or wider, within the bound.
A program may use at most 64 MiB of HBM per device.

```python
import math
import jax
import jax.numpy as jnp
from jax import lax

D = 4096
K = 4096
TILE = 128
HITS = 8
BANK = 64
MATS = 3
TOK = 128
NTEST = 1024
EXAMPLES = 16
TILES = 32
BLOCKS = 32


def set_ends(entries, own_key, low, top_value):
    longest = entries.shape.index(max(entries.shape))
    spots = []
    for shift in (0, 1):
        where = [jax.random.randint(jax.random.fold_in(own_key, axis), (), 0, length) for axis, length in enumerate(entries.shape)]
        where[longest] = (where[longest] + shift) % entries.shape[longest]
        spots.append(tuple(where))
    return entries.at[spots[0]].set(low).at[spots[1]].set(top_value)


def steps_of(stream_key, shape, pieces, low, high):
    loudness, own = 1.0, jax.random.fold_in(stream_key, 6)
    for dim, blocks in pieces:
        steps = jnp.exp(jax.random.uniform(jax.random.fold_in(own, dim), (blocks,), jnp.float32, low / len(pieces), high / len(pieces)))
        loudness = loudness * jnp.repeat(steps, shape[dim] // blocks).reshape([-1 if axis == dim else 1 for axis in range(len(shape))])
    return loudness


def normal_values(stream_key, dims, scale, bound, shards=(), kind=jnp.bfloat16):
    result = scale * jax.random.normal(stream_key, dims, jnp.float32)
    if shards:
        result = result * steps_of(stream_key, dims, shards, -0.22, 0.18)
    return jnp.clip(result, -bound, bound).astype(kind)


def setup_inputs(seed: int = 0) -> dict:
    streams_of = jax.random.split(jax.random.key(seed), 8)
    inputs = normal_values(streams_of[0], (EXAMPLES, TOK, D), 1.0, 6.0, ((0, 4), (2, 32)))
    cotangents = normal_values(streams_of[1], (MATS, EXAMPLES, TOK, D), 1.0, 6.0, ((1, 4), (3, 32)))
    jl_bank = normal_values(streams_of[2], (BANK, TILE, TILE), TILE ** -0.5, 0.5)
    jl_tiles = set_ends(jax.random.randint(streams_of[3], (MATS, TILES, TILES, HITS), 0, BANK), jax.random.fold_in(streams_of[3], 1), 0, BANK - 1).astype(jnp.int32)
    jl_blocks = set_ends(jax.random.randint(streams_of[4], (MATS, TILES, TILES, HITS), 0, BLOCKS), jax.random.fold_in(streams_of[4], 1), 0, BLOCKS - 1).astype(jnp.int32)
    jl_signs = set_ends(jax.random.randint(streams_of[5], (MATS, TILES, TILES, HITS), 0, 2), jax.random.fold_in(streams_of[5], 1), 0, 1).astype(jnp.int32)
    test_features = normal_values(streams_of[6], (NTEST, K), 1.0, 6.0, ((0, 4), (1, 32)))
    return dict(inputs=inputs, cotangents=cotangents, jl_bank=jl_bank, jl_tiles=jl_tiles, jl_blocks=jl_blocks, jl_signs=jl_signs, test_features=test_features)


def reference(inputs, cotangents, jl_bank, jl_tiles, jl_blocks, jl_signs, test_features):
    bank_float = jl_bank.astype(jnp.float32)
    sign_vals = (2 * jl_signs - 1).astype(jnp.float32)
    select = (jl_blocks[..., None] == jnp.arange(BLOCKS, dtype=jnp.int32)).astype(jnp.float32) * sign_vals[..., None]

    def per_example(example_pair):
        example_inputs, example_cots = example_pair
        input_tiles = example_inputs.astype(jnp.float32).reshape(TOK, TILES, TILE)
        cot_tiles = example_cots.astype(jnp.float32).reshape(MATS, TOK, TILES, TILE)

        def per_row(running, row_index):
            row_tiles = bank_float[jl_tiles[:, row_index]]
            products = jnp.einsum('mtjk,mjhka->mtjha', cot_tiles, row_tiles, precision=lax.Precision.HIGHEST).astype(jnp.bfloat16)
            products = lax.optimization_barrier(products).astype(jnp.float32)
            weighted = jnp.einsum('mtjha,ta->mjha', products, input_tiles[:, row_index], precision=lax.Precision.HIGHEST)
            added = jnp.einsum('mjha,mjhb->ba', weighted, select[:, row_index], precision=lax.Precision.HIGHEST)
            return (running + added, None)
        running, _ = lax.scan(per_row, jnp.zeros((BLOCKS, TILE), jnp.float32), jnp.arange(TILES, dtype=jnp.int32))
        return running
    raw_sums = lax.map(per_example, (inputs, jnp.moveaxis(cotangents, 1, 0)))
    features = raw_sums.reshape(EXAMPLES, K) / math.sqrt(TOK * MATS * HITS * D * D / (TILE * K))
    scores = jnp.dot(features, test_features.astype(jnp.float32).T, precision=lax.Precision.HIGHEST)
    return scores / math.sqrt(K)
```

```python
import functools
import math

import jax
import jax.numpy as jnp
from jax import lax
from jax.experimental import pallas as pl
from jax.experimental.pallas import tpu as pltpu
from jax.sharding import PartitionSpec as P

D = 4096
K = 4096
TILE = 128
HITS = 8
MATS = 3
TOK = 128
BANK = 64
BLOCKS = 32
EX = 4
ROWS = 8
COLS = 4
PAIRS = MATS * COLS // 2
GROUP = 32
BATCH = 2
MESH = pl.DeviceIdType.MESH
F32 = jnp.float32
BF16 = jnp.bfloat16
SCALE = 1.0 / (math.sqrt(TOK * MATS * HITS * D * D / (TILE * K)) * math.sqrt(K))
ORDER = (0, 2, 1, 3)


def dot(a, b):
    return lax.dot_general(a, b, (((1,), (0,)), ((), ())), preferred_element_type=F32)


def dot_nt(a, b):
    return lax.dot_general(a, b, (((1,), (1,)), ((), ())), preferred_element_type=F32)


def kernel(
    in_hbm, cot_hbm, bank_hbm, tiles_hbm, blocks_hbm, signs_hbm, test_hbm, out_ref,
    bank, bank_t, hits, cots, ins, left32, left, grads, quads, picked, count, tests,
    raw, raw_in, part, part_in, done,
    load_sem, own_sem, j_send, j_recv, i_send, i_recv, t_send, t_recv, ex_send, ex_recv,
):
    me = lax.axis_index("param")
    mx = lax.axis_index("ex")
    core = lax.rem(me, 2)
    y = lax.rem(me // 2, 4)
    z = me // 8

    def device(zz, yy, cc):
        return (zz * 4 + yy) * 2 + cc

    loads = [
        pltpu.make_async_copy(tiles_hbm, hits.at[0], load_sem.at[0]),
        pltpu.make_async_copy(blocks_hbm, hits.at[1], load_sem.at[1]),
        pltpu.make_async_copy(signs_hbm, hits.at[2], load_sem.at[2]),
        pltpu.make_async_copy(bank_hbm, bank, load_sem.at[3]),
        pltpu.make_async_copy(test_hbm, tests.at[mx], load_sem.at[4]),
    ]
    for copy in loads:
        copy.start()
    row_slot = [z * 2 + core, z * 2 + core, y * 2 + core, y * 2 + core]
    col_slot = [y, y, z, z]
    own = []
    for e in range(EX):
        own.append(pltpu.make_async_copy(in_hbm.at[e], ins.at[e, row_slot[e]], own_sem.at[e, 0]))
        own.append(pltpu.make_async_copy(cot_hbm.at[:, e], cots.at[e, col_slot[e]], own_sem.at[e, 1]))
    for copy in own:
        copy.start()

    barrier = pltpu.get_barrier_semaphore()

    def greet(d, carry):
        pl.semaphore_signal(
            barrier, inc=1, device_id={"param": lax.rem(me + d, GROUP)}, device_id_type=MESH
        )
        return carry

    lax.fori_loop(1, GROUP, greet, 0)
    for d in range(1, 4):
        pl.semaphore_signal(barrier, inc=1, device_id={"ex": lax.rem(mx + d, 4)}, device_id_type=MESH)
    pl.semaphore_wait(barrier, GROUP - 1 + 3)

    col_copies, row_copies = {}, {}
    for e in ORDER:
        along_y = e < 2
        for d in (1, 3, 2):
            if along_y:
                to = device(z, lax.rem(y + d, 4), core)
            else:
                to = device(lax.rem(z + d, 4), y, core)
            col_copies[e, d] = pltpu.make_async_remote_copy(
                src_ref=cot_hbm.at[:, e],
                dst_ref=cots.at[e, col_slot[e]],
                send_sem=j_send.at[e, d - 1],
                recv_sem=j_recv.at[e, d - 1],
                device_id={"param": to},
                device_id_type=MESH,
            )
            col_copies[e, d].start()
        for d in (1, 2, 3, 6, 7, 4, 5):
            other = lax.rem(core + d, 2)
            if along_y:
                to = device(lax.rem(z + d // 2, 4), y, other)
            else:
                to = device(z, lax.rem(y + d // 2, 4), other)
            row_copies[e, d] = pltpu.make_async_remote_copy(
                src_ref=in_hbm.at[e],
                dst_ref=ins.at[e, row_slot[e]],
                send_sem=i_send.at[e, d - 1],
                recv_sem=i_recv.at[e, d - 1],
                device_id={"param": to},
                device_id_type=MESH,
            )
            row_copies[e, d].start()
    test_copies = []
    for d in range(1, 4):
        copy = pltpu.make_async_remote_copy(
            src_ref=test_hbm,
            dst_ref=tests.at[mx],
            send_sem=t_send.at[d - 1],
            recv_sem=t_recv.at[d - 1],
            device_id={"ex": lax.rem(mx + d, 4)},
            device_id_type=MESH,
        )
        copy.start()
        test_copies.append(copy)

    for copy in loads:
        copy.wait()
    lane = lax.broadcasted_iota(jnp.int32, (HITS, TILE), 1)
    block_of_lane = lax.rem(lane, BLOCKS).astype(F32)
    quarter = lane // BLOCKS
    tile_of_row = lax.broadcasted_iota(jnp.int32, (BANK, 2 * TILE), 0).astype(F32)
    for kind in range(2):
        first, step = (z * 8 + core, 2) if kind == 0 else (y * 2 + core, 8)
        source = lax.broadcasted_iota(jnp.int32, (GROUP, COLS * TILE), 0)
        column = lax.broadcasted_iota(jnp.int32, (GROUP, COLS * TILE), 1) // TILE
        choose = jnp.where(source == first + step * column, 1.0, 0.0).astype(BF16)
        for m in range(MATS):
            spread = []
            for which in range(3):
                if kind == 0:
                    rows = [
                        hits[which, m, pl.ds(zz * 8 + y * 2, 2)].reshape(2 * HITS, GROUP)
                        for zz in range(4)
                    ]
                    values = jnp.concatenate(rows, axis=0)
                else:
                    values = hits[which, m, pl.ds(z * 8, ROWS)].reshape(ROWS * HITS, GROUP)
                spread.append(dot(values.astype(F32).astype(BF16), choose))

            def lanes_of(values, col, half):
                parts = [
                    values[(half * 4 + q) * HITS : (half * 4 + q + 1) * HITS, col * TILE : (col + 1) * TILE]
                    for q in range(4)
                ]
                low = jnp.where(quarter == 0, parts[0], parts[1])
                high = jnp.where(quarter == 2, parts[2], parts[3])
                return jnp.where(quarter < 2, low, high)

            for col in range(COLS):
                tile_rows, sign_rows = [], []
                for half in range(2):
                    tile, block, sign = [lanes_of(values, col, half) for values in spread]
                    tile_rows.append(jnp.where(block == block_of_lane, tile, -1.0))
                    sign_rows.append(2.0 * sign - 1.0)
                tile_rows = jnp.concatenate(tile_rows, axis=1)
                sign_rows = jnp.concatenate(sign_rows, axis=1)
                total = jnp.zeros((BANK, 2 * TILE), F32)
                for h in range(HITS):
                    total += jnp.where(
                        tile_of_row == tile_rows[h : h + 1, :], sign_rows[h : h + 1, :], 0.0
                    )
                at = (m * COLS + col) * BANK
                count[kind, at : at + BANK, :] = total.astype(BF16)

    def turn(r, carry):
        bank_t[pl.ds(r, TILE, stride=BANK), :] = bank[r].astype(F32).T
        return carry

    lax.fori_loop(0, BANK, turn, 0, unroll=4)
    for copy in own:
        copy.wait()

    raw[...] = jnp.zeros_like(raw)
    row_in_group = lax.rem(lax.broadcasted_iota(jnp.int32, (256, TILE), 0), ROWS)
    lane_group = lax.broadcasted_iota(jnp.int32, (256, TILE), 1) // BLOCKS
    upper = row_in_group >= 4
    keep = lane_group == lax.rem(row_in_group, 4)

    for first in range(0, EX, BATCH):
        batch = ORDER[first : first + BATCH]
        for slot, e in enumerate(batch):
            for d in range(1, 8):
                row_copies[e, d].wait_recv()

            def turn_rows(i, carry, e=e):
                left32[pl.ds(i, TILE, stride=ROWS), :] = ins[e, i].astype(F32).T
                return carry

            lax.fori_loop(0, ROWS, turn_rows, 0, unroll=4)
            left[...] = left32[...].astype(BF16)
            for d in range(1, 4):
                col_copies[e, d].wait_recv()

            def gradient(pair, carry, e=e, slot=slot):
                m = pair // 2
                col = lax.rem(pair, 2) * 2
                right = jnp.concatenate([cots[e, col, m], cots[e, col + 1, m]], axis=1)
                grads[slot, pair] = dot(left[...], right)
                return carry

            lax.fori_loop(0, PAIRS, gradient, 0)

        def project(a, carry):
            at = pl.multiple_of(a * ROWS, ROWS)
            lhs = jnp.concatenate(
                [grads[slot, pair, pl.ds(at, ROWS), :] for slot in range(BATCH) for pair in range(PAIRS)],
                axis=0,
            ).astype(BF16)
            tiles = bank_t[pl.ds(pl.multiple_of(a * BANK, BANK), BANK), :].astype(BF16)
            zero = jnp.zeros_like(tiles)
            weights = jnp.concatenate(
                [jnp.concatenate([tiles, zero], axis=1), jnp.concatenate([zero, tiles], axis=1)], axis=0
            )
            out = dot_nt(lhs, weights)
            for slot in range(BATCH):
                for pair in range(PAIRS):
                    src = (slot * PAIRS + pair) * ROWS
                    quads[slot, pl.ds(at, ROWS), pair * TILE : (pair + 1) * TILE] = out[src : src + ROWS]
            return carry

        lax.fori_loop(0, TILE, project, 0, unroll=4)

        for slot, e in enumerate(batch):
            kind = 0 if e < 2 else 1

            def select(chunk, carry, slot=slot, kind=kind):
                at = pl.multiple_of(chunk * 256, 256)
                sums = dot(quads[slot, pl.ds(at, 256), :].astype(BF16), count[kind])
                folded = jnp.where(upper, sums[:, TILE:], sums[:, :TILE])
                picked[pl.ds(at, 256), :] = jnp.where(keep, folded, 0.0)
                return carry

            lax.fori_loop(0, TILE * ROWS // 256, select, 0)
            total = picked[pl.ds(0, TILE, stride=ROWS), :]
            for i in range(1, ROWS):
                total += picked[pl.ds(i, TILE, stride=ROWS), :]
            turned = total.T
            folded = turned[0:32] + turned[32:64] + turned[64:96] + turned[96:128]
            raw[pl.ds(e, BLOCKS, stride=8), :] = folded

    def exchange(index, source, target):
        def copy(d):
            return pltpu.make_async_remote_copy(
                src_ref=source(lax.rem(me + d, GROUP)),
                dst_ref=target,
                send_sem=ex_send.at[index, d],
                recv_sem=ex_recv.at[index, d],
                device_id={"param": lax.rem(me + d, GROUP)},
                device_id_type=MESH,
            )

        def start(d, carry):
            copy(d).start()
            return carry

        def wait(d, carry):
            copy(d).wait_recv()
            return carry

        def drain(d, carry):
            copy(d).wait_send()
            return carry

        lax.fori_loop(1, GROUP, start, 0)
        lax.fori_loop(1, GROUP, wait, 0)
        return lambda: lax.fori_loop(1, GROUP, drain, 0)

    raw_in[me] = raw[pl.ds(pl.multiple_of(me * 8, 8), 8), :]
    drains = [
        exchange(0, lambda to: raw.at[pl.ds(pl.multiple_of(to * 8, 8), 8), :], raw_in.at[me])
    ]
    features = jnp.sum(raw_in[...], axis=0) * SCALE
    high = features.astype(BF16)
    low = (features - high.astype(F32)).astype(BF16)
    both = jnp.concatenate([high, low], axis=0)
    for copy in test_copies:
        copy.wait_recv()
    for quarter_of in range(4):
        scores = dot_nt(both, tests[quarter_of])
        scores = scores[:8] + scores[8:]
        for half in range(2):
            for e in range(EX):
                part[(quarter_of * 2 + half) * EX + e] = scores[e : e + 1, half * TILE : (half + 1) * TILE]
    part_in[me] = part[me]
    drains.append(exchange(1, lambda to: part.at[to], part_in.at[me]))
    done[me] = jnp.sum(part_in[...], axis=0)
    drains.append(exchange(2, lambda to: done.at[me], done.at[me]))
    for chunk in range(8):
        for e in range(EX):
            out_ref[e : e + 1, chunk * TILE : (chunk + 1) * TILE] = done[chunk * EX + e]
    for drain in drains:
        drain()
    for copy in list(col_copies.values()) + list(row_copies.values()) + test_copies:
        copy.wait_send()


def local(inputs, cotangents, jl_bank, jl_tiles, jl_blocks, jl_signs, test_features):
    turned = [jnp.transpose(a, (0, 1, 3, 2)) for a in (jl_tiles, jl_blocks, jl_signs)]
    anywhere = pl.BlockSpec(memory_space=pl.ANY)
    dma = pltpu.SemaphoreType.DMA
    return pl.pallas_call(
        kernel,
        out_shape=jax.ShapeDtypeStruct((EX, 1024), F32),
        in_specs=[anywhere] * 7,
        out_specs=pl.BlockSpec(memory_space=pltpu.VMEM),
        scratch_shapes=[
            pltpu.VMEM((BANK, TILE, TILE), BF16),
            pltpu.VMEM((TILE * BANK, TILE), F32),
            pltpu.VMEM((3, MATS, GROUP, HITS, GROUP), jnp.int32),
            pltpu.VMEM((EX, COLS, MATS, TOK, TILE), BF16),
            pltpu.VMEM((EX, ROWS, TOK, TILE), BF16),
            pltpu.VMEM((TILE * ROWS, TOK), F32),
            pltpu.VMEM((TILE * ROWS, TOK), BF16),
            pltpu.VMEM((BATCH, PAIRS, TILE * ROWS, 2 * TILE), F32),
            pltpu.VMEM((BATCH, TILE * ROWS, PAIRS * TILE), F32),
            pltpu.VMEM((TILE * ROWS, TILE), F32),
            pltpu.VMEM((2, MATS * COLS * BANK, 2 * TILE), BF16),
            pltpu.VMEM((4, 256, TILE), BF16),
            pltpu.VMEM((BLOCKS * 8, TILE), F32),
            pltpu.VMEM((GROUP, 8, TILE), F32),
            pltpu.VMEM((GROUP, 1, TILE), F32),
            pltpu.VMEM((GROUP, 1, TILE), F32),
            pltpu.VMEM((GROUP, 1, TILE), F32),
            dma((5,)),
            dma((EX, 2)),
            dma((EX, 3)),
            dma((EX, 3)),
            dma((EX, 7)),
            dma((EX, 7)),
            dma((3,)),
            dma((3,)),
            dma((3, GROUP)),
            dma((3, GROUP)),
        ],
        compiler_params=pltpu.CompilerParams(
            collective_id=0, has_side_effects=True, vmem_limit_bytes=56 * 1024 * 1024
        ),
        cost_estimate=pl.CostEstimate(flops=9_000_000_000, bytes_accessed=8_000_000, transcendentals=0),
    )(inputs, cotangents, jl_bank, *turned, test_features)


def solution(mesh):
    placed = (
        P("ex", None, "param"),
        P(None, "ex", None, "param"),
        P(),
        P(),
        P(),
        P(),
        P("ex", "param"),
    )
    return jax.shard_map(
        local, mesh=mesh, in_specs=placed, out_specs=P("ex", None), check_vma=False
    )
```

```python
import functools
import math

import jax
import jax.numpy as jnp
from jax import lax
from jax.experimental import pallas as pl
from jax.experimental.pallas import tpu as pltpu
from jax.sharding import PartitionSpec as P

D = 4096
K = 4096
TILE = 128
HITS = 8
MATS = 3
TOK = 128
BANK = 64
BLOCKS = 32
EX = 4
ROWS = 8
COLS = 4
PAIRS = MATS * COLS // 2
GROUP = 32
MESH = pl.DeviceIdType.MESH
F32 = jnp.float32
BF16 = jnp.bfloat16
SCALE = 1.0 / (math.sqrt(TOK * MATS * HITS * D * D / (TILE * K)) * math.sqrt(K))
ORDER = (0, 2, 1, 3)


def dot(a, b):
    return lax.dot_general(a, b, (((1,), (0,)), ((), ())), preferred_element_type=F32)


def dot_nt(a, b):
    return lax.dot_general(a, b, (((1,), (1,)), ((), ())), preferred_element_type=F32)


def count_hits(hits, count, z, y, core):
    lane = lax.broadcasted_iota(jnp.int32, (HITS, TILE), 1)
    block_of_lane = lax.rem(lane, BLOCKS).astype(F32)
    quarter = lane // BLOCKS
    tile_of_row = lax.broadcasted_iota(jnp.int32, (BANK, 2 * TILE), 0).astype(F32)
    for kind in range(2):
        first, step = (z * 8 + core, 2) if kind == 0 else (y * 2 + core, 8)
        source = lax.broadcasted_iota(jnp.int32, (GROUP, COLS * TILE), 0)
        column = lax.broadcasted_iota(jnp.int32, (GROUP, COLS * TILE), 1) // TILE
        choose = jnp.where(source == first + step * column, 1.0, 0.0).astype(BF16)
        for m in range(MATS):
            spread = []
            for which in range(3):
                if kind == 0:
                    rows = [
                        hits[which, m, pl.ds(zz * 8 + y * 2, 2)].reshape(2 * HITS, GROUP)
                        for zz in range(4)
                    ]
                    values = jnp.concatenate(rows, axis=0)
                else:
                    values = hits[which, m, pl.ds(z * 8, ROWS)].reshape(ROWS * HITS, GROUP)
                spread.append(dot(values.astype(F32).astype(BF16), choose))

            def lanes_of(values, col, half):
                parts = [
                    values[(half * 4 + q) * HITS : (half * 4 + q + 1) * HITS, col * TILE : (col + 1) * TILE]
                    for q in range(4)
                ]
                low = jnp.where(quarter == 0, parts[0], parts[1])
                high = jnp.where(quarter == 2, parts[2], parts[3])
                return jnp.where(quarter < 2, low, high)

            for col in range(COLS):
                tile_rows, sign_rows = [], []
                for half in range(2):
                    tile, block, sign = [lanes_of(values, col, half) for values in spread]
                    tile_rows.append(jnp.where(block == block_of_lane, tile, -1.0))
                    sign_rows.append(2.0 * sign - 1.0)
                tile_rows = jnp.concatenate(tile_rows, axis=1)
                sign_rows = jnp.concatenate(sign_rows, axis=1)
                total = jnp.zeros((BANK, 2 * TILE), F32)
                for h in range(HITS):
                    total += jnp.where(
                        tile_of_row == tile_rows[h : h + 1, :], sign_rows[h : h + 1, :], 0.0
                    )
                at = (m * COLS + col) * BANK
                count[kind, at : at + BANK, :] = total.astype(BF16)


def turn_bank(bank, bank_t):
    def turn(r, carry):
        bank_t[pl.ds(r, TILE, stride=BANK), :] = bank[r].astype(F32).T
        return carry

    lax.fori_loop(0, BANK, turn, 0, unroll=4)


def turn_rows(ins, left32, left, e):
    def turn(i, carry):
        left32[pl.ds(i, TILE, stride=ROWS), :] = ins[e, i].astype(F32).T
        return carry

    lax.fori_loop(0, ROWS, turn, 0, unroll=4)
    left[...] = left32[...].astype(BF16)


def gradient(left, cots, grads, e, slot):
    rows = left[...]
    for m in range(MATS):
        halves = []
        for col in range(0, COLS, 2):
            right = jnp.concatenate([cots[e, col, m], cots[e, col + 1, m]], axis=1)
            halves.append(dot(rows, right).reshape(TILE, ROWS, 2 * TILE))
        at = (slot * MATS + m) * 2 * ROWS
        grads[:, at : at + 2 * ROWS, :] = jnp.concatenate(halves, axis=1).astype(BF16)


def project(grads, bank_t, quads):
    def step(two, carry):
        outs = []
        for u in range(2):
            a = two * 2 + u
            tiles = bank_t[pl.ds(pl.multiple_of(a * BANK, BANK), BANK), :].astype(BF16)
            zero = jnp.zeros_like(tiles)
            weights = jnp.concatenate(
                [jnp.concatenate([tiles, zero], axis=1), jnp.concatenate([zero, tiles], axis=1)], axis=0
            )
            outs.append(dot_nt(grads[a], weights))
        at = pl.multiple_of(two * 2 * ROWS, 2 * ROWS)
        for slot in range(EX):
            for pair in range(PAIRS):
                src = (slot * PAIRS + pair) * ROWS
                both = jnp.concatenate([out[src : src + ROWS] for out in outs], axis=0)
                quads[slot, pl.ds(at, 2 * ROWS), pair * TILE : (pair + 1) * TILE] = both.astype(BF16)
        return carry

    lax.fori_loop(0, TILE // 2, step, 0, unroll=16)


def select(quads, count, picked, slot, kind):
    row_in_group = lax.rem(lax.broadcasted_iota(jnp.int32, (TILE * ROWS, TILE), 0), ROWS)
    lane_group = lax.broadcasted_iota(jnp.int32, (TILE * ROWS, TILE), 1) // BLOCKS
    sums = dot(quads[slot], count[kind])
    folded = jnp.where(row_in_group >= 4, sums[:, TILE:], sums[:, :TILE])
    picked[...] = jnp.where(lane_group == lax.rem(row_in_group, 4), folded, 0.0)
    total = picked[pl.ds(0, TILE, stride=ROWS), :]
    for i in range(1, ROWS):
        total += picked[pl.ds(i, TILE, stride=ROWS), :]
    turned = total.T
    return turned[0:32] + turned[32:64] + turned[64:96] + turned[96:128]


class Ring:
    def __init__(self, source, slots, slot_of, send, recv, pos, to):
        self.slots, self.slot_of, self.send, self.recv = slots, slot_of, send, recv
        self.pos, self.to, self.source = pos, to, source
        self.copies = []

    def _copy(self, src, dst, index, direction):
        copy = pltpu.make_async_remote_copy(
            src_ref=src,
            dst_ref=dst,
            send_sem=self.send.at[index],
            recv_sem=self.recv.at[index],
            device_id={"param": self.to(direction)},
            device_id_type=MESH,
        )
        copy.start()
        self.copies.append(copy)

    def slot(self, offset):
        return self.slot_of(lax.rem(self.pos + offset + 4, 4))

    def start(self):
        mine = self.slots.at[self.slot(0)]
        self._copy(self.source, mine, 0, 1)
        self._copy(self.source, mine, 1, -1)

    def hand_on(self):
        half = TOK // 2
        for way in range(2):
            self.copies[way].wait_recv()
            came_from = self.slots.at[self.slot(-1 if way == 0 else 1)]
            tokens = pl.ds(way * half, half)
            piece = came_from.at[:, tokens] if len(came_from.shape) == 3 else came_from.at[tokens]
            self._copy(piece, piece, 2 + way, 1 if way == 0 else -1)

    def finish(self):
        self.copies[2].wait_recv()
        self.copies[3].wait_recv()


def kernel(
    in_hbm, cot_hbm, bank_hbm, tiles_hbm, blocks_hbm, signs_hbm, test_hbm, out_ref,
    bank, bank_t, hits, cots, ins, left32, left, grads, quads, picked, count, tests,
    raw, raw_in, part, part_in, done,
    load_sem, own_sem, j_send, j_recv, i_send, i_recv, p_send, p_recv, t_send, t_recv, ex_send, ex_recv,
):
    me = lax.axis_index("param")
    mx = lax.axis_index("ex")
    core = lax.rem(me, 2)
    y = lax.rem(me // 2, 4)
    z = me // 8

    def device(zz, yy, cc):
        return (zz * 4 + yy) * 2 + cc

    loads = [
        pltpu.make_async_copy(tiles_hbm, hits.at[0], load_sem.at[0]),
        pltpu.make_async_copy(blocks_hbm, hits.at[1], load_sem.at[1]),
        pltpu.make_async_copy(signs_hbm, hits.at[2], load_sem.at[2]),
        pltpu.make_async_copy(bank_hbm, bank, load_sem.at[3]),
        pltpu.make_async_copy(test_hbm, tests.at[mx], load_sem.at[4]),
    ]
    for copy in loads:
        copy.start()
    row_slot = [z * 2 + core, z * 2 + core, y * 2 + core, y * 2 + core]
    col_slot = [y, y, z, z]
    own = []
    for e in range(EX):
        own.append(pltpu.make_async_copy(in_hbm.at[e], ins.at[e, row_slot[e]], own_sem.at[e, 0]))
        own.append(pltpu.make_async_copy(cot_hbm.at[:, e], cots.at[e, col_slot[e]], own_sem.at[e, 1]))
    for copy in own:
        copy.start()

    barrier = pltpu.get_barrier_semaphore()

    def greet(d, carry):
        pl.semaphore_signal(
            barrier, inc=1, device_id={"param": lax.rem(me + d, GROUP)}, device_id_type=MESH
        )
        return carry

    lax.fori_loop(1, GROUP, greet, 0)
    for d in range(1, 4):
        pl.semaphore_signal(barrier, inc=1, device_id={"ex": lax.rem(mx + d, 4)}, device_id_type=MESH)
    pl.semaphore_wait(barrier, GROUP - 1 + 3)

    cols, rows, relays = {}, {}, {}
    sibling = device(z, y, 1 - core)

    def along_y(direction):
        return device(z, lax.rem(y + direction + 4, 4), core)

    def along_z(direction):
        return device(lax.rem(z + direction + 4, 4), y, core)

    def relay(e, index, offset):
        slot = rows[e].slot(offset)
        copy = pltpu.make_async_remote_copy(
            src_ref=ins.at[e, slot],
            dst_ref=ins.at[e, slot],
            send_sem=p_send.at[e, index],
            recv_sem=p_recv.at[e, index],
            device_id={"param": sibling},
            device_id_type=MESH,
        )
        copy.start()
        relays[e, index] = copy

    for e in ORDER:
        col_pos, col_to, row_pos, row_to = (y, along_y, z, along_z) if e < 2 else (z, along_z, y, along_y)
        cols[e] = Ring(
            cot_hbm.at[:, e], cots.at[e], lambda pos: pos, j_send.at[e], j_recv.at[e], col_pos, col_to
        )
        rows[e] = Ring(
            in_hbm.at[e], ins.at[e], lambda pos: pos * 2 + core, i_send.at[e], i_recv.at[e], row_pos, row_to
        )
        rows[e].start()
        cols[e].start()
    test_copies = []
    for d in range(1, 4):
        copy = pltpu.make_async_remote_copy(
            src_ref=test_hbm,
            dst_ref=tests.at[mx],
            send_sem=t_send.at[d - 1],
            recv_sem=t_recv.at[d - 1],
            device_id={"ex": lax.rem(mx + d, 4)},
            device_id_type=MESH,
        )
        copy.start()
        test_copies.append(copy)

    for copy in own:
        copy.wait()
    for e in ORDER:
        relay(e, 0, 0)
    for copy in loads:
        copy.wait()

    def hand_on(e):
        rows[e].hand_on()
        relay(e, 1, -1)
        relay(e, 2, 1)
        cols[e].hand_on()

    count_hits(hits, count, z, y, core)
    hand_on(ORDER[0])
    hand_on(ORDER[1])
    turn_bank(bank, bank_t)
    hand_on(ORDER[2])
    hand_on(ORDER[3])
    raw[...] = jnp.zeros_like(raw)
    for e in ORDER:
        rows[e].finish()
        relay(e, 3, 2)
    for slot, e in enumerate(ORDER):
        for index in range(4):
            relays[e, index].wait_recv()
        turn_rows(ins, left32, left, e)
        cols[e].finish()
        gradient(left, cots, grads, e, slot)
    project(grads, bank_t, quads)
    for slot, e in enumerate(ORDER):
        raw[pl.ds(e, BLOCKS, stride=8), :] = select(quads, count, picked, slot, 0 if e < 2 else 1)

    def exchange(index, source, target):
        def copy(d):
            return pltpu.make_async_remote_copy(
                src_ref=source(lax.rem(me + d, GROUP)),
                dst_ref=target,
                send_sem=ex_send.at[index, d],
                recv_sem=ex_recv.at[index, d],
                device_id={"param": lax.rem(me + d, GROUP)},
                device_id_type=MESH,
            )

        def start(d, carry):
            copy(d).start()
            return carry

        def wait(d, carry):
            copy(d).wait_recv()
            return carry

        def drain(d, carry):
            copy(d).wait_send()
            return carry

        lax.fori_loop(1, GROUP, start, 0)
        lax.fori_loop(1, GROUP, wait, 0)
        return lambda: lax.fori_loop(1, GROUP, drain, 0)

    raw_in[me] = raw[pl.ds(pl.multiple_of(me * 8, 8), 8), :]
    drains = [
        exchange(0, lambda to: raw.at[pl.ds(pl.multiple_of(to * 8, 8), 8), :], raw_in.at[me])
    ]
    features = jnp.sum(raw_in[...], axis=0) * SCALE
    high = features.astype(BF16)
    low = (features - high.astype(F32)).astype(BF16)
    both = jnp.concatenate([high, low], axis=0)
    for copy in test_copies:
        copy.wait_recv()
    for quarter_of in range(4):
        scores = dot_nt(both, tests[quarter_of])
        scores = scores[:8] + scores[8:]
        for half in range(2):
            for e in range(EX):
                part[(quarter_of * 2 + half) * EX + e] = scores[e : e + 1, half * TILE : (half + 1) * TILE]
    part_in[me] = part[me]
    drains.append(exchange(1, lambda to: part.at[to], part_in.at[me]))
    done[me] = jnp.sum(part_in[...], axis=0)
    drains.append(exchange(2, lambda to: done.at[me], done.at[me]))
    for chunk in range(8):
        for e in range(EX):
            out_ref[e : e + 1, chunk * TILE : (chunk + 1) * TILE] = done[chunk * EX + e]
    for drain in drains:
        drain()
    for ring in list(cols.values()) + list(rows.values()):
        for copy in ring.copies:
            copy.wait_send()
    for copy in list(relays.values()) + test_copies:
        copy.wait_send()


def local(inputs, cotangents, jl_bank, jl_tiles, jl_blocks, jl_signs, test_features):
    turned = [jnp.transpose(a, (0, 1, 3, 2)) for a in (jl_tiles, jl_blocks, jl_signs)]
    anywhere = pl.BlockSpec(memory_space=pl.ANY)
    dma = pltpu.SemaphoreType.DMA
    return pl.pallas_call(
        kernel,
        out_shape=jax.ShapeDtypeStruct((EX, 1024), F32),
        in_specs=[anywhere] * 7,
        out_specs=pl.BlockSpec(memory_space=pltpu.VMEM),
        scratch_shapes=[
            pltpu.VMEM((BANK, TILE, TILE), BF16),
            pltpu.VMEM((TILE * BANK, TILE), F32),
            pltpu.VMEM((3, MATS, GROUP, HITS, GROUP), jnp.int32),
            pltpu.VMEM((EX, COLS, MATS, TOK, TILE), BF16),
            pltpu.VMEM((EX, ROWS, TOK, TILE), BF16),
            pltpu.VMEM((TILE * ROWS, TOK), F32),
            pltpu.VMEM((TILE * ROWS, TOK), BF16),
            pltpu.VMEM((TILE, EX * PAIRS * ROWS, 2 * TILE), BF16),
            pltpu.VMEM((EX, TILE * ROWS, PAIRS * TILE), BF16),
            pltpu.VMEM((TILE * ROWS, TILE), F32),
            pltpu.VMEM((2, MATS * COLS * BANK, 2 * TILE), BF16),
            pltpu.VMEM((4, 256, TILE), BF16),
            pltpu.VMEM((BLOCKS * 8, TILE), F32),
            pltpu.VMEM((GROUP, 8, TILE), F32),
            pltpu.VMEM((GROUP, 1, TILE), F32),
            pltpu.VMEM((GROUP, 1, TILE), F32),
            pltpu.VMEM((GROUP, 1, TILE), F32),
            dma((5,)),
            dma((EX, 2)),
            dma((EX, 4)),
            dma((EX, 4)),
            dma((EX, 4)),
            dma((EX, 4)),
            dma((EX, 4)),
            dma((EX, 4)),
            dma((3,)),
            dma((3,)),
            dma((3, GROUP)),
            dma((3, GROUP)),
        ],
        compiler_params=pltpu.CompilerParams(
            collective_id=0, has_side_effects=True, vmem_limit_bytes=56 * 1024 * 1024
        ),
        cost_estimate=pl.CostEstimate(flops=9_000_000_000, bytes_accessed=8_000_000, transcendentals=0),
    )(inputs, cotangents, jl_bank, *turned, test_features)


def solution(mesh):
    placed = (
        P("ex", None, "param"),
        P(None, "ex", None, "param"),
        P(),
        P(),
        P(),
        P(),
        P("ex", "param"),
    )
    return jax.shard_map(
        local, mesh=mesh, in_specs=placed, out_specs=P("ex", None), check_vma=False
    )
```

```python
import functools
import math

import jax
import jax.numpy as jnp
from jax import lax
from jax.experimental import pallas as pl
from jax.experimental.pallas import tpu as pltpu
from jax.sharding import PartitionSpec as P

D = 4096
K = 4096
TILE = 128
HITS = 8
MATS = 3
TOK = 128
BANK = 64
BLOCKS = 32
EX = 4
ROWS = 8
COLS = 4
PAIRS = MATS * COLS // 2
GROUP = 32
MESH = pl.DeviceIdType.MESH
F32 = jnp.float32
BF16 = jnp.bfloat16
SCALE = 1.0 / (math.sqrt(TOK * MATS * HITS * D * D / (TILE * K)) * math.sqrt(K))
ORDER = (0, 2, 1, 3)


def dot(a, b):
    return lax.dot_general(a, b, (((1,), (0,)), ((), ())), preferred_element_type=F32)


def dot_nt(a, b):
    return lax.dot_general(a, b, (((1,), (1,)), ((), ())), preferred_element_type=F32)


def count_hits(hits, count, z, y, core):
    lane = lax.broadcasted_iota(jnp.int32, (HITS, TILE), 1)
    block_of_lane = lax.rem(lane, BLOCKS).astype(F32)
    quarter = lane // BLOCKS
    tile_of_row = lax.broadcasted_iota(jnp.int32, (BANK, 2 * TILE), 0).astype(F32)
    for kind in range(2):
        first, step = (z * 8 + core, 2) if kind == 0 else (y * 2 + core, 8)
        source = lax.broadcasted_iota(jnp.int32, (GROUP, COLS * TILE), 0)
        column = lax.broadcasted_iota(jnp.int32, (GROUP, COLS * TILE), 1) // TILE
        choose = jnp.where(source == first + step * column, 1.0, 0.0).astype(BF16)
        for m in range(MATS):
            spread = []
            for which in range(3):
                if kind == 0:
                    rows = [
                        hits[which, m, pl.ds(zz * 8 + y * 2, 2)].reshape(2 * HITS, GROUP)
                        for zz in range(4)
                    ]
                    values = jnp.concatenate(rows, axis=0)
                else:
                    values = hits[which, m, pl.ds(z * 8, ROWS)].reshape(ROWS * HITS, GROUP)
                spread.append(dot(values.astype(F32).astype(BF16), choose))

            def lanes_of(values, col, half):
                parts = [
                    values[(half * 4 + q) * HITS : (half * 4 + q + 1) * HITS, col * TILE : (col + 1) * TILE]
                    for q in range(4)
                ]
                low = jnp.where(quarter == 0, parts[0], parts[1])
                high = jnp.where(quarter == 2, parts[2], parts[3])
                return jnp.where(quarter < 2, low, high)

            for col in range(COLS):
                tile_rows, sign_rows = [], []
                for half in range(2):
                    tile, block, sign = [lanes_of(values, col, half) for values in spread]
                    tile_rows.append(jnp.where(block == block_of_lane, tile, -1.0))
                    sign_rows.append(2.0 * sign - 1.0)
                tile_rows = jnp.concatenate(tile_rows, axis=1)
                sign_rows = jnp.concatenate(sign_rows, axis=1)
                total = jnp.zeros((BANK, 2 * TILE), F32)
                for h in range(HITS):
                    total += jnp.where(
                        tile_of_row == tile_rows[h : h + 1, :], sign_rows[h : h + 1, :], 0.0
                    )
                at = (m * COLS + col) * BANK
                count[kind, at : at + BANK, :] = total.astype(BF16)


def turn_bank(bank, bank_t):
    def turn(r, carry):
        bank_t[pl.ds(r, TILE, stride=BANK), :] = bank[r].astype(F32).T
        return carry

    lax.fori_loop(0, BANK, turn, 0, unroll=4)


def turn_rows(ins, left32, left, e):
    def turn(i, carry):
        left32[pl.ds(i, TILE, stride=ROWS), :] = ins[e, i].astype(F32).T
        return carry

    lax.fori_loop(0, ROWS, turn, 0, unroll=4)
    left[...] = left32[...].astype(BF16)


def gradient(left, cots, grads, e, slot):
    rows = left[...]
    for m in range(MATS):
        halves = []
        for col in range(0, COLS, 2):
            right = jnp.concatenate([cots[e, col, m], cots[e, col + 1, m]], axis=1)
            halves.append(dot(rows, right).reshape(TILE, ROWS, 2 * TILE))
        at = (slot * MATS + m) * 2 * ROWS
        grads[:, at : at + 2 * ROWS, :] = jnp.concatenate(halves, axis=1).astype(BF16)


def project(grads, bank_t, quads):
    def step(two, carry):
        outs = []
        for u in range(2):
            a = two * 2 + u
            tiles = bank_t[pl.ds(pl.multiple_of(a * BANK, BANK), BANK), :].astype(BF16)
            zero = jnp.zeros_like(tiles)
            weights = jnp.concatenate(
                [jnp.concatenate([tiles, zero], axis=1), jnp.concatenate([zero, tiles], axis=1)], axis=0
            )
            outs.append(dot_nt(grads[a], weights))
        at = pl.multiple_of(two * 2 * ROWS, 2 * ROWS)
        for slot in range(EX):
            for pair in range(PAIRS):
                src = (slot * PAIRS + pair) * ROWS
                both = jnp.concatenate([out[src : src + ROWS] for out in outs], axis=0)
                quads[slot, pl.ds(at, 2 * ROWS), pair * TILE : (pair + 1) * TILE] = both.astype(BF16)
        return carry

    lax.fori_loop(0, TILE // 2, step, 0, unroll=16)


def select(quads, count, picked, slot, kind):
    row_in_group = lax.rem(lax.broadcasted_iota(jnp.int32, (TILE * ROWS, TILE), 0), ROWS)
    lane_group = lax.broadcasted_iota(jnp.int32, (TILE * ROWS, TILE), 1) // BLOCKS
    sums = dot(quads[slot], count[kind])
    folded = jnp.where(row_in_group >= 4, sums[:, TILE:], sums[:, :TILE])
    picked[...] = jnp.where(lane_group == lax.rem(row_in_group, 4), folded, 0.0)
    total = picked[pl.ds(0, TILE, stride=ROWS), :]
    for i in range(1, ROWS):
        total += picked[pl.ds(i, TILE, stride=ROWS), :]
    turned = total.T
    return turned[0:32] + turned[32:64] + turned[64:96] + turned[96:128]


class Ring:
    def __init__(self, source, place, send, recv, pos, to):
        self.source, self.place, self.send, self.recv = source, place, send, recv
        self.pos, self.to = pos, to
        self.copies = []

    def _copy(self, src, dst, index, direction):
        copy = pltpu.make_async_remote_copy(
            src_ref=src,
            dst_ref=dst,
            send_sem=self.send.at[index],
            recv_sem=self.recv.at[index],
            device_id={"param": self.to(direction)},
            device_id_type=MESH,
        )
        copy.start()
        self.copies.append(copy)

    def at(self, offset):
        return self.place(lax.rem(self.pos + offset + 4, 4))

    def start(self):
        self._copy(self.source, self.at(0), 0, 1)
        self._copy(self.source, self.at(0), 1, -1)

    def hand_on(self):
        half = TOK // 2
        for way in range(2):
            self.copies[way].wait_recv()
            piece = self.at(-1 if way == 0 else 1).at[:, pl.ds(way * half, half)]
            self._copy(piece, piece, 2 + way, 1 if way == 0 else -1)

    def finish(self):
        self.copies[2].wait_recv()
        self.copies[3].wait_recv()


def kernel(
    in_hbm, cot_hbm, bank_hbm, tiles_hbm, blocks_hbm, signs_hbm, test_hbm, out_ref,
    bank, bank_t, hits, cots, ins, left32, left, grads, quads, picked, count, tests,
    raw, raw_in, part, part_in, done,
    load_sem, own_sem, j_send, j_recv, i_send, i_recv, p_send, p_recv, t_send, t_recv, ex_send, ex_recv, ready,
):
    me = lax.axis_index("param")
    mx = lax.axis_index("ex")
    core = lax.rem(me, 2)
    y = lax.rem(me // 2, 4)
    z = me // 8

    def device(zz, yy, cc):
        return (zz * 4 + yy) * 2 + cc

    def along_y(direction):
        return device(z, lax.rem(y + direction + 4, 4), core)

    def along_z(direction):
        return device(lax.rem(z + direction + 4, 4), y, core)

    sibling = device(z, y, 1 - core)

    barrier = pltpu.get_barrier_semaphore()
    for to in (along_y(1), along_y(-1), along_z(1), along_z(-1), sibling):
        pl.semaphore_signal(barrier, inc=1, device_id={"param": to}, device_id_type=MESH)
    for d in range(1, 4):
        pl.semaphore_signal(barrier, inc=1, device_id={"ex": lax.rem(mx + d, 4)}, device_id_type=MESH)

    loads = [
        pltpu.make_async_copy(tiles_hbm, hits.at[0], load_sem.at[0]),
        pltpu.make_async_copy(blocks_hbm, hits.at[1], load_sem.at[1]),
        pltpu.make_async_copy(signs_hbm, hits.at[2], load_sem.at[2]),
        pltpu.make_async_copy(bank_hbm, bank, load_sem.at[3]),
    ]
    for copy in loads:
        copy.start()
    own = [pltpu.make_async_copy(test_hbm, tests.at[mx], load_sem.at[4])]
    for kind in range(2):
        pair = pl.ds(2 * kind, 2)
        col_pos, row_pos = (y, z) if kind == 0 else (z, y)
        own.append(
            pltpu.make_async_copy(
                in_hbm.at[pair], ins.at[pair, row_pos * 2 + core], own_sem.at[kind]
            )
        )
        for e in (2 * kind, 2 * kind + 1):
            own.append(
                pltpu.make_async_copy(cot_hbm.at[:, e], cots.at[e, col_pos], own_sem.at[2 + e])
            )
    for copy in own:
        copy.start()

    for copy in loads[:3]:
        copy.wait()
    count_hits(hits, count, z, y, core)
    loads[3].wait()
    turn_bank(bank, bank_t)
    raw[...] = jnp.zeros_like(raw)
    pl.semaphore_wait(barrier, 5 + 3)

    cols, rows, relays, tests_out = {}, {}, {}, []

    def relay(kind, index, offset):
        place = rows[kind].at(offset)
        copy = pltpu.make_async_remote_copy(
            src_ref=rows[kind].source if index == 0 else place,
            dst_ref=place,
            send_sem=p_send.at[kind, index],
            recv_sem=p_recv.at[kind, index],
            device_id={"param": sibling},
            device_id_type=MESH,
        )
        copy.start()
        relays[kind, index] = copy

    for kind in range(2):
        pair = pl.ds(2 * kind, 2)
        pos, to = (z, along_z) if kind == 0 else (y, along_y)
        rows[kind] = Ring(
            in_hbm.at[pair], lambda at, pair=pair: ins.at[pair, at * 2 + core],
            i_send.at[kind], i_recv.at[kind], pos, to,
        )
        rows[kind].start()
    for e in ORDER:
        pos, to = (y, along_y) if e < 2 else (z, along_z)
        cols[e] = Ring(
            cot_hbm.at[:, e], lambda at, e=e: cots.at[e, at], j_send.at[e], j_recv.at[e], pos, to
        )
        cols[e].start()
    for kind in range(2):
        relay(kind, 0, 0)
    for d in range(1, 4):
        copy = pltpu.make_async_remote_copy(
            src_ref=test_hbm,
            dst_ref=tests.at[mx],
            send_sem=t_send.at[d - 1],
            recv_sem=t_recv.at[d - 1],
            device_id={"ex": lax.rem(mx + d, 4)},
            device_id_type=MESH,
        )
        copy.start()
        tests_out.append(copy)
    for copy in own:
        copy.wait()

    for kind in range(2):
        rows[kind].hand_on()
        relay(kind, 1, -1)
        relay(kind, 2, 1)
    cols[ORDER[0]].hand_on()
    cols[ORDER[1]].hand_on()
    for kind in range(2):
        rows[kind].finish()
        relay(kind, 3, 2)
    cols[ORDER[2]].hand_on()
    for slot, e in enumerate(ORDER):
        if slot == 1:
            cols[ORDER[3]].hand_on()
        kind = e // 2
        if e % 2 == 0:
            for index in range(4):
                relays[kind, index].wait_recv()
        turn_rows(ins, left32, left, e)
        cols[e].finish()
        gradient(left, cots, grads, e, slot)
    pl.semaphore_signal(ready, inc=1, device_id={"param": sibling}, device_id_type=MESH)
    project(grads, bank_t, quads)
    for slot, e in enumerate(ORDER):
        raw[pl.ds(e, BLOCKS, stride=8), :] = select(quads, count, picked, slot, e // 2)

    def exchange(index, source, incoming):
        for d in range(1, GROUP):
            to = lax.rem(me + d, GROUP)
            pltpu.make_async_remote_copy(
                src_ref=source(to),
                dst_ref=incoming.at[me],
                send_sem=ex_send.at[index],
                recv_sem=ex_recv.at[index],
                device_id={"param": to},
                device_id_type=MESH,
            ).start()
        others = incoming.at[pl.ds(0, GROUP - 1)]
        pltpu.make_async_copy(others, others, ex_recv.at[index]).wait()
        return lambda: pltpu.make_async_copy(others, others, ex_send.at[index]).wait()

    pl.semaphore_wait(ready, 1)
    raw_in[me] = raw[pl.ds(pl.multiple_of(me * 8, 8), 8), :]
    drains = [
        exchange(0, lambda to: raw.at[pl.ds(pl.multiple_of(to * 8, 8), 8), :], raw_in)
    ]
    features = jnp.sum(raw_in[...], axis=0) * SCALE
    high = features.astype(BF16)
    low = (features - high.astype(F32)).astype(BF16)
    both = jnp.concatenate([high, low], axis=0)
    for copy in tests_out:
        copy.wait_recv()
    for quarter_of in range(4):
        scores = dot_nt(both, tests[quarter_of])
        scores = scores[:8] + scores[8:]
        for half in range(2):
            for e in range(EX):
                part[(quarter_of * 2 + half) * EX + e] = scores[e : e + 1, half * TILE : (half + 1) * TILE]
    part_in[me] = part[me]
    drains.append(exchange(1, lambda to: part.at[to], part_in))
    done[me] = jnp.sum(part_in[...], axis=0)
    drains.append(exchange(2, lambda to: done.at[me], done))
    for chunk in range(8):
        for e in range(EX):
            out_ref[e : e + 1, chunk * TILE : (chunk + 1) * TILE] = done[chunk * EX + e]
    for drain in drains:
        drain()
    for ring in list(cols.values()) + list(rows.values()):
        for copy in ring.copies:
            copy.wait_send()
    for copy in list(relays.values()) + tests_out:
        copy.wait_send()


def local(inputs, cotangents, jl_bank, jl_tiles, jl_blocks, jl_signs, test_features):
    turned = [jnp.transpose(a, (0, 1, 3, 2)) for a in (jl_tiles, jl_blocks, jl_signs)]
    anywhere = pl.BlockSpec(memory_space=pl.ANY)
    dma = pltpu.SemaphoreType.DMA
    return pl.pallas_call(
        kernel,
        out_shape=jax.ShapeDtypeStruct((EX, 1024), F32),
        in_specs=[anywhere] * 7,
        out_specs=pl.BlockSpec(memory_space=pltpu.VMEM),
        scratch_shapes=[
            pltpu.VMEM((BANK, TILE, TILE), BF16),
            pltpu.VMEM((TILE * BANK, TILE), F32),
            pltpu.VMEM((3, MATS, GROUP, HITS, GROUP), jnp.int32),
            pltpu.VMEM((EX, COLS, MATS, TOK, TILE), BF16),
            pltpu.VMEM((EX, ROWS, TOK, TILE), BF16),
            pltpu.VMEM((TILE * ROWS, TOK), F32),
            pltpu.VMEM((TILE * ROWS, TOK), BF16),
            pltpu.VMEM((TILE, EX * PAIRS * ROWS, 2 * TILE), BF16),
            pltpu.VMEM((EX, TILE * ROWS, PAIRS * TILE), BF16),
            pltpu.VMEM((TILE * ROWS, TILE), F32),
            pltpu.VMEM((2, MATS * COLS * BANK, 2 * TILE), BF16),
            pltpu.VMEM((4, 256, TILE), BF16),
            pltpu.VMEM((BLOCKS * 8, TILE), F32),
            pltpu.VMEM((GROUP, 8, TILE), F32),
            pltpu.VMEM((GROUP, 1, TILE), F32),
            pltpu.VMEM((GROUP, 1, TILE), F32),
            pltpu.VMEM((GROUP, 1, TILE), F32),
            dma((5,)),
            dma((2 + EX,)),
            dma((EX, 4)),
            dma((EX, 4)),
            dma((2, 4)),
            dma((2, 4)),
            dma((2, 4)),
            dma((2, 4)),
            dma((3,)),
            dma((3,)),
            dma((3,)),
            dma((3,)),
            pltpu.SemaphoreType.REGULAR,
        ],
        compiler_params=pltpu.CompilerParams(
            collective_id=0, has_side_effects=True, vmem_limit_bytes=56 * 1024 * 1024
        ),
        cost_estimate=pl.CostEstimate(flops=9_000_000_000, bytes_accessed=8_000_000, transcendentals=0),
    )(inputs, cotangents, jl_bank, *turned, test_features)


def solution(mesh):
    placed = (
        P("ex", None, "param"),
        P(None, "ex", None, "param"),
        P(),
        P(),
        P(),
        P(),
        P("ex", "param"),
    )
    return jax.shard_map(
        local, mesh=mesh, in_specs=placed, out_specs=P("ex", None), check_vma=False
    )
```

```python
import functools
import math

import jax
import jax.numpy as jnp
from jax import lax
from jax.experimental import pallas as pl
from jax.experimental.pallas import tpu as pltpu
from jax.sharding import PartitionSpec as P

D = 4096
K = 4096
TILE = 128
HITS = 8
MATS = 3
TOK = 128
BANK = 64
BLOCKS = 32
EX = 4
ROWS = 8
COLS = 4
PAIRS = MATS * COLS // 2
GROUP = 32
BATCH = 2
MESH = pl.DeviceIdType.MESH
F32 = jnp.float32
BF16 = jnp.bfloat16
SCALE = 1.0 / (math.sqrt(TOK * MATS * HITS * D * D / (TILE * K)) * math.sqrt(K))
ORDER = (0, 2, 1, 3)


def dot(a, b):
    return lax.dot_general(a, b, (((1,), (0,)), ((), ())), preferred_element_type=F32)


def dot_nt(a, b):
    return lax.dot_general(a, b, (((1,), (1,)), ((), ())), preferred_element_type=F32)


def count_hits(hits, count, z, y, core):
    lane = lax.broadcasted_iota(jnp.int32, (HITS, TILE), 1)
    block_of_lane = lax.rem(lane, BLOCKS).astype(F32)
    quarter = lane // BLOCKS
    tile_of_row = lax.broadcasted_iota(jnp.int32, (BANK, 2 * TILE), 0).astype(F32)
    for kind in range(2):
        first, step = (z * 8 + core, 2) if kind == 0 else (y * 2 + core, 8)
        source = lax.broadcasted_iota(jnp.int32, (GROUP, COLS * TILE), 0)
        column = lax.broadcasted_iota(jnp.int32, (GROUP, COLS * TILE), 1) // TILE
        choose = jnp.where(source == first + step * column, 1.0, 0.0).astype(BF16)
        for m in range(MATS):
            spread = []
            for which in range(3):
                if kind == 0:
                    rows = [
                        hits[which, m, pl.ds(zz * 8 + y * 2, 2)].reshape(2 * HITS, GROUP)
                        for zz in range(4)
                    ]
                    values = jnp.concatenate(rows, axis=0)
                else:
                    values = hits[which, m, pl.ds(z * 8, ROWS)].reshape(ROWS * HITS, GROUP)
                spread.append(dot(values.astype(F32).astype(BF16), choose))

            def lanes_of(values, col, half):
                parts = [
                    values[(half * 4 + q) * HITS : (half * 4 + q + 1) * HITS, col * TILE : (col + 1) * TILE]
                    for q in range(4)
                ]
                low = jnp.where(quarter == 0, parts[0], parts[1])
                high = jnp.where(quarter == 2, parts[2], parts[3])
                return jnp.where(quarter < 2, low, high)

            for col in range(COLS):
                tile_rows, sign_rows = [], []
                for half in range(2):
                    tile, block, sign = [lanes_of(values, col, half) for values in spread]
                    tile_rows.append(jnp.where(block == block_of_lane, tile, -1.0))
                    sign_rows.append(2.0 * sign - 1.0)
                tile_rows = jnp.concatenate(tile_rows, axis=1)
                sign_rows = jnp.concatenate(sign_rows, axis=1)
                total = jnp.zeros((BANK, 2 * TILE), F32)
                for h in range(HITS):
                    total += jnp.where(
                        tile_of_row == tile_rows[h : h + 1, :], sign_rows[h : h + 1, :], 0.0
                    )
                at = (m * COLS + col) * BANK
                count[kind, at : at + BANK, :] = total.astype(BF16)


def turn_bank(bank, bank_t):
    def turn(r, carry):
        bank_t[pl.ds(r, TILE, stride=BANK), :] = bank[r].astype(F32).T
        return carry

    lax.fori_loop(0, BANK, turn, 0, unroll=4)


def turn_rows(ins, left32, left, e):
    def turn(i, carry):
        left32[pl.ds(i, TILE, stride=ROWS), :] = ins[e, i].astype(F32).T
        return carry

    lax.fori_loop(0, ROWS, turn, 0, unroll=4)
    left[...] = left32[...].astype(BF16)


def spread_bank(bank_t, weights):
    lower = lax.broadcasted_iota(jnp.int32, (TILE, 2 * BANK), 1) < BANK

    def step(a, carry):
        tiles = bank_t[pl.ds(pl.multiple_of(a * BANK, BANK), BANK), :]
        turned = jnp.concatenate([tiles, tiles], axis=0).T
        weights[a, 0:TILE] = jnp.where(lower, turned, 0.0).astype(BF16)
        weights[a, TILE:] = jnp.where(lower, 0.0, turned).astype(BF16)
        return carry

    lax.fori_loop(0, TILE, step, 0, unroll=4)


def gradient(left, cots, grads, e, slot):
    rows = left[...]
    for m in range(MATS):
        halves = []
        for col in range(0, COLS, 2):
            right = jnp.concatenate([cots[e, col, m], cots[e, col + 1, m]], axis=1)
            halves.append(dot(rows, right).reshape(TILE, ROWS, 2 * TILE))
        at = (slot * MATS + m) * 2 * ROWS
        grads[:, at : at + 2 * ROWS, :] = jnp.concatenate(halves, axis=1).astype(BF16)


def project(grads, weights, quads):
    def step(two, carry):
        outs = [dot(grads[two * 2 + u], weights[two * 2 + u]) for u in range(2)]
        at = pl.multiple_of(two * 2 * ROWS, 2 * ROWS)
        for slot in range(BATCH):
            for pair in range(PAIRS):
                src = (slot * PAIRS + pair) * ROWS
                both = jnp.concatenate([out[src : src + ROWS] for out in outs], axis=0)
                quads[slot, pl.ds(at, 2 * ROWS), pair * TILE : (pair + 1) * TILE] = both.astype(BF16)
        return carry

    lax.fori_loop(0, TILE // 2, step, 0, unroll=16)


def select(quads, count, picked, slot, kind):
    row_in_group = lax.rem(lax.broadcasted_iota(jnp.int32, (TILE * ROWS, TILE), 0), ROWS)
    lane_group = lax.broadcasted_iota(jnp.int32, (TILE * ROWS, TILE), 1) // BLOCKS
    sums = dot(quads[slot], count[kind])
    folded = jnp.where(row_in_group >= 4, sums[:, TILE:], sums[:, :TILE])
    picked[...] = jnp.where(lane_group == lax.rem(row_in_group, 4), folded, 0.0)
    total = picked[pl.ds(0, TILE, stride=ROWS), :]
    for i in range(1, ROWS):
        total += picked[pl.ds(i, TILE, stride=ROWS), :]
    turned = total.T
    return turned[0:32] + turned[32:64] + turned[64:96] + turned[96:128]


def kernel(
    in_hbm, cot_hbm, bank_hbm, tiles_hbm, blocks_hbm, signs_hbm, test_hbm, out_ref,
    bank, bank_t, weights, hits, cots, ins, left32, left, grads, quads, picked, count, tests,
    raw, sums_out, sums_in, done,
    load_sem, own_sem, j_send, j_recv, i_send, i_recv, p_send, p_recv, t_send, t_recv, ex_send, ex_recv,
):
    me = lax.axis_index("param")
    mx = lax.axis_index("ex")
    core = lax.rem(me, 2)
    y = lax.rem(me // 2, 4)
    z = me // 8

    def device(zz, yy, cc):
        return (zz * 4 + yy) * 2 + cc

    def along_y(distance):
        return device(z, lax.rem(y + distance, 4), core)

    def along_z(distance):
        return device(lax.rem(z + distance, 4), y, core)

    sibling = device(z, y, 1 - core)
    family, member = me // 4, lax.rem(me, 4)
    alone = member == mx

    barrier = pltpu.get_barrier_semaphore()

    def greet(**to):
        pl.semaphore_signal(barrier, inc=1, device_id=to, device_id_type=MESH)

    for d in (1, 3, 2):
        greet(param=along_y(d))
        greet(param=along_z(d))
    greet(param=sibling)
    for j in range(4):
        sender = family * 4 + j

        @pl.when(jnp.logical_or(sender != me, member != mx))
        def _(sender=sender):
            greet(param=sender, ex=member)

    loads = [
        pltpu.make_async_copy(tiles_hbm, hits.at[0], load_sem.at[0]),
        pltpu.make_async_copy(blocks_hbm, hits.at[1], load_sem.at[1]),
        pltpu.make_async_copy(signs_hbm, hits.at[2], load_sem.at[2]),
        pltpu.make_async_copy(bank_hbm, bank, load_sem.at[3]),
    ]
    for copy in loads:
        copy.start()
    own = []
    for kind in range(2):
        pair = pl.ds(2 * kind, 2)
        col_pos, row_pos = (y, z) if kind == 0 else (z, y)
        own.append(
            pltpu.make_async_copy(
                in_hbm.at[pair], ins.at[pair, row_pos * 2 + core], own_sem.at[kind]
            )
        )
        for e in (2 * kind, 2 * kind + 1):
            own.append(
                pltpu.make_async_copy(cot_hbm.at[:, e], cots.at[e, col_pos], own_sem.at[2 + e])
            )
    for copy in own:
        copy.start()

    for copy in loads[:3]:
        copy.wait()
    count_hits(hits, count, z, y, core)
    loads[3].wait()
    turn_bank(bank, bank_t)
    pl.semaphore_wait(barrier, 7 + jnp.where(alone, 3, 4))

    def send(src, dst, send_sem, recv_sem, **to):
        copy = pltpu.make_async_remote_copy(
            src_ref=src, dst_ref=dst, send_sem=send_sem, recv_sem=recv_sem, device_id=to, device_id_type=MESH
        )
        copy.start()
        return copy

    cols, rows, relays = {}, {}, {}

    def rings(e):
        return ((y, along_y), (z, along_z)) if e < 2 else ((z, along_z), (y, along_y))

    def send_tiles(batch):
        for e in batch:
            pos, to = rings(e)[1]
            place = ins.at[e, pos * 2 + core]
            for d in (2, 1, 3):
                rows[e, d] = send(in_hbm.at[e], place, i_send.at[e, d], i_recv.at[e, d], param=to(d))
            relays[e, 0] = send(in_hbm.at[e], place, p_send.at[e, 0], p_recv.at[e, 0], param=sibling)
        for e in batch:
            pos, to = rings(e)[0]
            for d in (2, 1, 3):
                cols[e, d] = send(
                    cot_hbm.at[:, e], cots.at[e, pos], j_send.at[e, d], j_recv.at[e, d], param=to(d)
                )

    def relay_rows(batch):
        for e in batch:
            pos = rings(e)[1][0]
            for d in (1, 3, 2):
                rows[e, d].wait_recv()
                place = ins.at[e, lax.rem(pos + 4 - d, 4) * 2 + core]
                relays[e, d] = send(place, place, p_send.at[e, d], p_recv.at[e, d], param=sibling)

    def gradients(batch):
        for slot, e in enumerate(batch):
            for index in range(4):
                relays[e, index].wait_recv()
            turn_rows(ins, left32, left, e)
            for d in (1, 3, 2):
                cols[e, d].wait_recv()
            gradient(left, cots, grads, e, slot)

    def finish(batch):
        project(grads, weights, quads)
        for slot, e in enumerate(batch):
            raw[pl.ds(e, BLOCKS, stride=EX), :] = select(quads, count, picked, slot, e // 2)

    early, late = ORDER[:BATCH], ORDER[BATCH:]
    send_tiles(early)
    spread_bank(bank_t, weights)
    for copy in own:
        copy.wait()
    relay_rows(early)
    send_tiles(late)
    tests_out = [
        send(
            test_hbm, tests.at[member], t_send.at[d], t_recv.at[member],
            param=family * 4 + mx, ex=lax.rem(mx + d, 4),
        )
        for d in range(1, 4)
    ]
    test_here = pltpu.make_async_copy(test_hbm, tests.at[member], t_recv.at[member])
    test_near = pltpu.make_async_remote_copy(
        src_ref=test_hbm,
        dst_ref=tests.at[member],
        send_sem=t_send.at[0],
        recv_sem=t_recv.at[member],
        device_id={"param": family * 4 + mx, "ex": mx},
        device_id_type=MESH,
    )

    @pl.when(alone)
    def _():
        test_here.start()

    @pl.when(jnp.logical_not(alone))
    def _():
        test_near.start()

    gradients(early)
    relay_rows(late)
    finish(early)
    gradients(late)
    finish(late)
    sums_out[...] = raw[...].astype(BF16).reshape(8, 4 * EX, TILE)

    others = sorted(
        [(dz, dy, dc) for dz in range(4) for dy in range(4) for dc in range(2)][1:],
        key=lambda d: -(min(d[0], 4 - d[0]) + min(d[1], 4 - d[1])),
    )

    def exchange(index, source, incoming, beside=None):
        for dz, dy, dc in others:
            to = device(lax.rem(z + dz, 4), lax.rem(y + dy, 4), lax.rem(core + dc, 2))
            send(source(to), incoming.at[me], ex_send.at[index], ex_recv.at[index], param=to)
        if beside is not None:
            beside()
        rest = incoming.at[pl.ds(0, GROUP - 1)]
        pltpu.make_async_copy(rest, rest, ex_recv.at[index]).wait()
        return pltpu.make_async_copy(rest, rest, ex_send.at[index])

    def drain():
        for j in range(4):
            pltpu.make_async_copy(tests.at[j], tests.at[j], t_recv.at[j]).wait()
        for copy in [*cols.values(), *rows.values(), *relays.values(), *tests_out]:
            copy.wait_send()

        @pl.when(jnp.logical_not(alone))
        def _():
            test_near.wait_send()

    sums_in[me] = sums_out[family]
    sums_sent = exchange(0, lambda to: sums_out.at[to // 4], sums_in, drain)
    features = jnp.sum(sums_in[...].astype(F32), axis=0) * SCALE
    high = features.astype(BF16)
    low = (features - high.astype(F32)).astype(BF16)
    scores = jnp.zeros((2 * EX, 256), F32)
    for j in range(4):
        both = jnp.concatenate([high[j * EX : (j + 1) * EX], low[j * EX : (j + 1) * EX]], axis=0)
        scores += dot_nt(both, tests[j])
    done[me] = scores[:EX] + scores[EX:]
    scores_sent = exchange(1, lambda to: done.at[me], done, sums_sent.wait)
    for j in range(4):
        total = done[j]
        for other in range(1, 8):
            total += done[other * 4 + j]
        out_ref[:, j * 256 : (j + 1) * 256] = total
    scores_sent.wait()


def local(inputs, cotangents, jl_bank, jl_tiles, jl_blocks, jl_signs, test_features):
    turned = [jnp.transpose(a, (0, 1, 3, 2)) for a in (jl_tiles, jl_blocks, jl_signs)]
    anywhere = pl.BlockSpec(memory_space=pl.ANY)
    dma = pltpu.SemaphoreType.DMA
    return pl.pallas_call(
        kernel,
        out_shape=jax.ShapeDtypeStruct((EX, 1024), F32),
        in_specs=[anywhere] * 7,
        out_specs=pl.BlockSpec(memory_space=pltpu.VMEM),
        scratch_shapes=[
            pltpu.VMEM((BANK, TILE, TILE), BF16),
            pltpu.VMEM((TILE * BANK, TILE), F32),
            pltpu.VMEM((TILE, 2 * TILE, 2 * BANK), BF16),
            pltpu.VMEM((3, MATS, GROUP, HITS, GROUP), jnp.int32),
            pltpu.VMEM((EX, COLS, MATS, TOK, TILE), BF16),
            pltpu.VMEM((EX, ROWS, TOK, TILE), BF16),
            pltpu.VMEM((TILE * ROWS, TOK), F32),
            pltpu.VMEM((TILE * ROWS, TOK), BF16),
            pltpu.VMEM((TILE, BATCH * PAIRS * ROWS, 2 * TILE), BF16),
            pltpu.VMEM((BATCH, TILE * ROWS, PAIRS * TILE), BF16),
            pltpu.VMEM((TILE * ROWS, TILE), F32),
            pltpu.VMEM((2, MATS * COLS * BANK, 2 * TILE), BF16),
            pltpu.VMEM((4, 256, TILE), BF16),
            pltpu.VMEM((BLOCKS * EX, TILE), F32),
            pltpu.VMEM((8, 4 * EX, TILE), BF16),
            pltpu.VMEM((GROUP, 4 * EX, TILE), BF16),
            pltpu.VMEM((GROUP, EX, 256), F32),
            dma((4,)),
            dma((2 + EX,)),
            dma((EX, 4)),
            dma((EX, 4)),
            dma((EX, 4)),
            dma((EX, 4)),
            dma((EX, 4)),
            dma((EX, 4)),
            dma((4,)),
            dma((4,)),
            dma((2,)),
            dma((2,)),
        ],
        compiler_params=pltpu.CompilerParams(
            collective_id=0, has_side_effects=True, vmem_limit_bytes=56 * 1024 * 1024
        ),
        cost_estimate=pl.CostEstimate(flops=9_000_000_000, bytes_accessed=8_000_000, transcendentals=0),
    )(inputs, cotangents, jl_bank, *turned, test_features)


def solution(mesh):
    placed = (
        P("ex", None, "param"),
        P(None, "ex", None, "param"),
        P(),
        P(),
        P(),
        P(),
        P("ex", "param"),
    )
    return jax.shard_map(
        local, mesh=mesh, in_specs=placed, out_specs=P("ex", None), check_vma=False
    )
```

```python
import functools
import math

import jax
import jax.numpy as jnp
from jax import lax
from jax.experimental import pallas as pl
from jax.experimental.pallas import tpu as pltpu
from jax.sharding import PartitionSpec as P

D = 4096
K = 4096
TILE = 128
HITS = 8
MATS = 3
TOK = 128
BANK = 64
BLOCKS = 32
EX = 4
ROWS = 8
COLS = 4
PAIRS = MATS * COLS // 2
GROUP = 32
BATCH = 2
UNROLL = 32
MESH = pl.DeviceIdType.MESH
F32 = jnp.float32
BF16 = jnp.bfloat16
SCALE = 1.0 / (math.sqrt(TOK * MATS * HITS * D * D / (TILE * K)) * math.sqrt(K))
ORDER = (0, 2, 1, 3)


def dot(a, b):
    return lax.dot_general(a, b, (((1,), (0,)), ((), ())), preferred_element_type=F32)


def count_hits(hits, count, z, y, core):
    lane = lax.broadcasted_iota(jnp.int32, (HITS, TILE), 1)
    block_of_lane = lax.rem(lane, BLOCKS).astype(F32)
    quarter = lane // BLOCKS
    tile_of_row = lax.broadcasted_iota(jnp.int32, (BANK, 2 * TILE), 0).astype(F32)
    for kind in range(2):
        first, step = (z * 8 + core, 2) if kind == 0 else (y * 2 + core, 8)
        source = lax.broadcasted_iota(jnp.int32, (GROUP, COLS * TILE), 0)
        column = lax.broadcasted_iota(jnp.int32, (GROUP, COLS * TILE), 1) // TILE
        choose = jnp.where(source == first + step * column, 1.0, 0.0).astype(BF16)
        for m in range(MATS):
            spread = []
            for which in range(3):
                if kind == 0:
                    rows = [
                        hits[which, m, pl.ds(zz * 8 + y * 2, 2)].reshape(2 * HITS, GROUP)
                        for zz in range(4)
                    ]
                    values = jnp.concatenate(rows, axis=0)
                else:
                    values = hits[which, m, pl.ds(z * 8, ROWS)].reshape(ROWS * HITS, GROUP)
                spread.append(dot(values.astype(F32).astype(BF16), choose))

            def lanes_of(values, col, half):
                parts = [
                    values[(half * 4 + q) * HITS : (half * 4 + q + 1) * HITS, col * TILE : (col + 1) * TILE]
                    for q in range(4)
                ]
                low = jnp.where(quarter == 0, parts[0], parts[1])
                high = jnp.where(quarter == 2, parts[2], parts[3])
                return jnp.where(quarter < 2, low, high)

            for col in range(COLS):
                tile_rows, sign_rows = [], []
                for half in range(2):
                    tile, block, sign = [lanes_of(values, col, half) for values in spread]
                    tile_rows.append(jnp.where(block == block_of_lane, tile, -1.0))
                    sign_rows.append(2.0 * sign - 1.0)
                tile_rows = jnp.concatenate(tile_rows, axis=1)
                sign_rows = jnp.concatenate(sign_rows, axis=1)
                total = jnp.zeros((BANK, 2 * TILE), F32)
                for h in range(HITS):
                    total += jnp.where(
                        tile_of_row == tile_rows[h : h + 1, :], sign_rows[h : h + 1, :], 0.0
                    )
                at = (m * COLS + col) * BANK
                count[kind, at : at + BANK, :] = total.astype(BF16)


def turn_bank(bank, bank_t):
    def turn(r, carry):
        bank_t[pl.ds(r, TILE, stride=BANK), :] = bank[r].astype(F32).T
        return carry

    lax.fori_loop(0, BANK, turn, 0, unroll=4)


def turn_rows(ins, left32, left, e, slot):
    for i in range(ROWS):
        left32[slot, pl.ds(i, TILE, stride=ROWS), :] = ins[e, i].astype(F32).T
    left[slot] = left32[slot].astype(BF16)


def spread_bank(bank_t, weights):
    lower = lax.broadcasted_iota(jnp.int32, (TILE, 2 * BANK), 1) < BANK

    def step(a, carry):
        tiles = bank_t[pl.ds(pl.multiple_of(a * BANK, BANK), BANK), :]
        turned = jnp.concatenate([tiles, tiles], axis=0).T
        weights[a, 0:TILE] = jnp.where(lower, turned, 0.0).astype(BF16)
        weights[a, TILE:] = jnp.where(lower, 0.0, turned).astype(BF16)
        return carry

    lax.fori_loop(0, TILE, step, 0, unroll=4)


def gradient(left, cots, grads, e, slot):
    rows = left[slot]
    for m in range(MATS):
        halves = []
        for col in range(0, COLS, 2):
            right = jnp.concatenate([cots[e, col, m], cots[e, col + 1, m]], axis=1)
            halves.append(dot(rows, right).reshape(TILE, ROWS, 2 * TILE))
        at = (slot * MATS + m) * 2 * ROWS
        grads[:, at : at + 2 * ROWS, :] = jnp.concatenate(halves, axis=1).astype(BF16)


def project(grads, weights, quads):
    def step(two, carry):
        outs = [dot(grads[two * 2 + u], weights[two * 2 + u]) for u in range(2)]
        at = pl.multiple_of(two * 2 * ROWS, 2 * ROWS)
        for slot in range(BATCH):
            for pair in range(PAIRS):
                src = (slot * PAIRS + pair) * ROWS
                both = jnp.concatenate([out[src : src + ROWS] for out in outs], axis=0)
                quads[slot, pl.ds(at, 2 * ROWS), pair * TILE : (pair + 1) * TILE] = both.astype(BF16)
        return carry

    lax.fori_loop(0, TILE // 2, step, 0, unroll=UNROLL)


def select(quads, count, picked, slot, kind):
    row_in_group = lax.rem(lax.broadcasted_iota(jnp.int32, (TILE * ROWS, TILE), 0), ROWS)
    lane_group = lax.broadcasted_iota(jnp.int32, (TILE * ROWS, TILE), 1) // BLOCKS
    sums = dot(quads[slot], count[kind])
    folded = jnp.where(row_in_group >= 4, sums[:, TILE:], sums[:, :TILE])
    picked[slot] = jnp.where(lane_group == lax.rem(row_in_group, 4), folded, 0.0)
    total = picked[slot, pl.ds(0, TILE, stride=ROWS), :]
    for i in range(1, ROWS):
        total += picked[slot, pl.ds(i, TILE, stride=ROWS), :]
    turned = total.T
    return turned[0:32] + turned[32:64] + turned[64:96] + turned[96:128]


def kernel(
    in_hbm, cot_hbm, bank_hbm, tiles_hbm, blocks_hbm, signs_hbm, test_hbm, out_ref,
    bank, bank_t, weights, hits, cots, ins, left32, left, grads, quads, picked, count, tests, tests_t,
    raw, sums_out, sums_in, done,
    load_sem, own_sem, j_send, j_recv, i_send, i_recv, p_send, p_recv, t_send, t_recv, ex_send, ex_recv,
):
    me = lax.axis_index("param")
    mx = lax.axis_index("ex")
    core = lax.rem(me, 2)
    y = lax.rem(me // 2, 4)
    z = me // 8

    def device(zz, yy, cc):
        return (zz * 4 + yy) * 2 + cc

    def along_y(distance):
        return device(z, lax.rem(y + distance, 4), core)

    def along_z(distance):
        return device(lax.rem(z + distance, 4), y, core)

    sibling = device(z, y, 1 - core)
    family, member = me // 4, lax.rem(me, 4)
    alone = member == mx

    barrier = pltpu.get_barrier_semaphore()

    def greet(**to):
        pl.semaphore_signal(barrier, inc=1, device_id=to, device_id_type=MESH)

    for d in (1, 3, 2):
        greet(param=along_y(d))
        greet(param=along_z(d))
    greet(param=sibling)
    for j in range(4):
        sender = family * 4 + j

        @pl.when(jnp.logical_or(sender != me, member != mx))
        def _(sender=sender):
            greet(param=sender, ex=member)

    loads = [
        pltpu.make_async_copy(tiles_hbm, hits.at[0], load_sem.at[0]),
        pltpu.make_async_copy(blocks_hbm, hits.at[1], load_sem.at[1]),
        pltpu.make_async_copy(signs_hbm, hits.at[2], load_sem.at[2]),
        pltpu.make_async_copy(bank_hbm, bank, load_sem.at[3]),
    ]
    for copy in loads:
        copy.start()
    own = []
    for kind in range(2):
        pair = pl.ds(2 * kind, 2)
        col_pos, row_pos = (y, z) if kind == 0 else (z, y)
        own.append(
            pltpu.make_async_copy(
                in_hbm.at[pair], ins.at[pair, row_pos * 2 + core], own_sem.at[kind]
            )
        )
        for e in (2 * kind, 2 * kind + 1):
            own.append(
                pltpu.make_async_copy(cot_hbm.at[:, e], cots.at[e, col_pos], own_sem.at[2 + e])
            )
    for copy in own:
        copy.start()

    for copy in loads[:3]:
        copy.wait()
    count_hits(hits, count, z, y, core)
    pl.semaphore_wait(barrier, 7 + jnp.where(alone, 3, 4))

    def send(src, dst, send_sem, recv_sem, **to):
        copy = pltpu.make_async_remote_copy(
            src_ref=src, dst_ref=dst, send_sem=send_sem, recv_sem=recv_sem, device_id=to, device_id_type=MESH
        )
        copy.start()
        return copy

    cols, rows, relays = {}, {}, {}

    def rings(e):
        return ((y, along_y), (z, along_z)) if e < 2 else ((z, along_z), (y, along_y))

    def send_tiles(batch):
        for e in batch:
            pos, to = rings(e)[1]
            place = ins.at[e, pos * 2 + core]
            for d in (2, 1, 3):
                rows[e, d] = send(in_hbm.at[e], place, i_send.at[e, d], i_recv.at[e, d], param=to(d))
            relays[e, 0] = send(in_hbm.at[e], place, p_send.at[e, 0], p_recv.at[e, 0], param=sibling)
        for e in batch:
            pos, to = rings(e)[0]
            for d in (2, 1, 3):
                cols[e, d] = send(
                    cot_hbm.at[:, e], cots.at[e, pos], j_send.at[e, d], j_recv.at[e, d], param=to(d)
                )

    def relay_rows(batch):
        for e in batch:
            pos = rings(e)[1][0]
            for d in (1, 3, 2):
                rows[e, d].wait_recv()
                place = ins.at[e, lax.rem(pos + 4 - d, 4) * 2 + core]
                relays[e, d] = send(place, place, p_send.at[e, d], p_recv.at[e, d], param=sibling)

    def gradients(batch):
        for slot, e in enumerate(batch):
            for index in range(4):
                relays[e, index].wait_recv()
            turn_rows(ins, left32, left, e, slot)
        for slot, e in enumerate(batch):
            for d in (1, 3, 2):
                cols[e, d].wait_recv()
        for slot, e in enumerate(batch):
            gradient(left, cots, grads, e, slot)

    def finish(batch):
        project(grads, weights, quads)
        for slot, e in enumerate(batch):
            raw[pl.ds(e, BLOCKS, stride=EX), :] = select(quads, count, picked, slot, e // 2)

    early, late = ORDER[:BATCH], ORDER[BATCH:]
    send_tiles(early)
    loads[3].wait()
    turn_bank(bank, bank_t)
    spread_bank(bank_t, weights)
    for copy in own:
        copy.wait()
    relay_rows(early)
    send_tiles(late)
    tests_out = [
        send(
            test_hbm, tests.at[member], t_send.at[d], t_recv.at[member],
            param=family * 4 + mx, ex=lax.rem(mx + d, 4),
        )
        for d in range(1, 4)
    ]
    test_here = pltpu.make_async_copy(test_hbm, tests.at[member], t_recv.at[member])
    test_near = pltpu.make_async_remote_copy(
        src_ref=test_hbm,
        dst_ref=tests.at[member],
        send_sem=t_send.at[0],
        recv_sem=t_recv.at[member],
        device_id={"param": family * 4 + mx, "ex": mx},
        device_id_type=MESH,
    )

    @pl.when(alone)
    def _():
        test_here.start()

    @pl.when(jnp.logical_not(alone))
    def _():
        test_near.start()

    gradients(early)
    relay_rows(late)
    finish(early)
    gradients(late)
    finish(late)
    sums_out[...] = raw[...].astype(BF16).reshape(8, 4 * EX, TILE)

    others = sorted(
        [(dz, dy, dc) for dz in range(4) for dy in range(4) for dc in range(2)][1:],
        key=lambda d: -(min(d[0], 4 - d[0]) + min(d[1], 4 - d[1])),
    )

    def exchange(index, source, incoming, beside=None):
        for dz, dy, dc in others:
            to = device(lax.rem(z + dz, 4), lax.rem(y + dy, 4), lax.rem(core + dc, 2))
            send(source(to), incoming.at[me], ex_send.at[index], ex_recv.at[index], param=to)
        if beside is not None:
            beside()
        rest = incoming.at[pl.ds(0, GROUP - 1)]
        pltpu.make_async_copy(rest, rest, ex_recv.at[index]).wait()
        return pltpu.make_async_copy(rest, rest, ex_send.at[index])

    def drain():
        for j in range(4):
            pltpu.make_async_copy(tests.at[j], tests.at[j], t_recv.at[j]).wait()
            for half in range(2):
                piece = tests[j, half * TILE : (half + 1) * TILE].astype(F32).T
                tests_t[j, :, half * TILE : (half + 1) * TILE] = piece.astype(BF16)
        for copy in [*cols.values(), *rows.values(), *relays.values(), *tests_out]:
            copy.wait_send()

        @pl.when(jnp.logical_not(alone))
        def _():
            test_near.wait_send()

    sums_in[me] = sums_out[family]
    sums_sent = exchange(0, lambda to: sums_out.at[to // 4], sums_in, drain)
    features = jnp.sum(sums_in[...].astype(F32), axis=0) * SCALE
    high = features.astype(BF16)
    low = (features - high.astype(F32)).astype(BF16)
    scores = jnp.zeros((2 * EX, 256), F32)
    for j in range(4):
        both = jnp.concatenate([high[j * EX : (j + 1) * EX], low[j * EX : (j + 1) * EX]], axis=0)
        scores += dot(both, tests_t[j])
    done[me] = scores[:EX] + scores[EX:]
    scores_sent = exchange(1, lambda to: done.at[me], done, sums_sent.wait)
    for j in range(4):
        total = done[j]
        for other in range(1, 8):
            total += done[other * 4 + j]
        out_ref[:, j * 256 : (j + 1) * 256] = total
    scores_sent.wait()


def local(inputs, cotangents, jl_bank, jl_tiles, jl_blocks, jl_signs, test_features):
    turned = [jnp.transpose(a, (0, 1, 3, 2)) for a in (jl_tiles, jl_blocks, jl_signs)]
    anywhere = pl.BlockSpec(memory_space=pl.ANY)
    dma = pltpu.SemaphoreType.DMA
    return pl.pallas_call(
        kernel,
        out_shape=jax.ShapeDtypeStruct((EX, 1024), F32),
        in_specs=[anywhere] * 7,
        out_specs=pl.BlockSpec(memory_space=pltpu.VMEM),
        scratch_shapes=[
            pltpu.VMEM((BANK, TILE, TILE), BF16),
            pltpu.VMEM((TILE * BANK, TILE), F32),
            pltpu.VMEM((TILE, 2 * TILE, 2 * BANK), BF16),
            pltpu.VMEM((3, MATS, GROUP, HITS, GROUP), jnp.int32),
            pltpu.VMEM((EX, COLS, MATS, TOK, TILE), BF16),
            pltpu.VMEM((EX, ROWS, TOK, TILE), BF16),
            pltpu.VMEM((BATCH, TILE * ROWS, TOK), F32),
            pltpu.VMEM((BATCH, TILE * ROWS, TOK), BF16),
            pltpu.VMEM((TILE, BATCH * PAIRS * ROWS, 2 * TILE), BF16),
            pltpu.VMEM((BATCH, TILE * ROWS, PAIRS * TILE), BF16),
            pltpu.VMEM((BATCH, TILE * ROWS, TILE), F32),
            pltpu.VMEM((2, MATS * COLS * BANK, 2 * TILE), BF16),
            pltpu.VMEM((4, 256, TILE), BF16),
            pltpu.VMEM((4, TILE, 256), BF16),
            pltpu.VMEM((BLOCKS * EX, TILE), F32),
            pltpu.VMEM((8, 4 * EX, TILE), BF16),
            pltpu.VMEM((GROUP, 4 * EX, TILE), BF16),
            pltpu.VMEM((GROUP, EX, 256), F32),
            dma((4,)),
            dma((2 + EX,)),
            dma((EX, 4)),
            dma((EX, 4)),
            dma((EX, 4)),
            dma((EX, 4)),
            dma((EX, 4)),
            dma((EX, 4)),
            dma((4,)),
            dma((4,)),
            dma((2,)),
            dma((2,)),
        ],
        compiler_params=pltpu.CompilerParams(
            collective_id=0, has_side_effects=True, vmem_limit_bytes=56 * 1024 * 1024
        ),
        cost_estimate=pl.CostEstimate(flops=9_000_000_000, bytes_accessed=8_000_000, transcendentals=0),
    )(inputs, cotangents, jl_bank, *turned, test_features)


def solution(mesh):
    placed = (
        P("ex", None, "param"),
        P(None, "ex", None, "param"),
        P(),
        P(),
        P(),
        P(),
        P("ex", "param"),
    )
    return jax.shard_map(
        local, mesh=mesh, in_specs=placed, out_specs=P("ex", None), check_vma=False
    )
```

```python
import functools
import math

import jax
import jax.numpy as jnp
from jax import lax
from jax.experimental import pallas as pl
from jax.experimental.pallas import tpu as pltpu
from jax.sharding import PartitionSpec as P

D = 4096
K = 4096
TILE = 128
HITS = 8
MATS = 3
TOK = 128
BANK = 64
BLOCKS = 32
EX = 4
ROWS = 8
COLS = 4
PAIRS = MATS * COLS // 2
GROUP = 32
BATCH = 2
UNROLL = 32
MESH = pl.DeviceIdType.MESH
F32 = jnp.float32
BF16 = jnp.bfloat16
SCALE = 1.0 / (math.sqrt(TOK * MATS * HITS * D * D / (TILE * K)) * math.sqrt(K))
ORDER = (0, 2, 1, 3)


def dot(a, b):
    return lax.dot_general(a, b, (((1,), (0,)), ((), ())), preferred_element_type=F32)


def count_hits(hits, count, z, y, core):
    lane = lax.broadcasted_iota(jnp.int32, (HITS, TILE), 1)
    block_of_lane = lax.rem(lane, BLOCKS).astype(F32)
    quarter = lane // BLOCKS
    tile_of_row = lax.broadcasted_iota(jnp.int32, (BANK, 2 * TILE), 0).astype(F32)
    for kind in range(2):
        first, step = (z * 8 + core, 2) if kind == 0 else (y * 2 + core, 8)
        source = lax.broadcasted_iota(jnp.int32, (GROUP, COLS * TILE), 0)
        column = lax.broadcasted_iota(jnp.int32, (GROUP, COLS * TILE), 1) // TILE
        choose = jnp.where(source == first + step * column, 1.0, 0.0).astype(BF16)
        for m in range(MATS):
            spread = []
            for which in range(3):
                if kind == 0:
                    rows = [
                        hits[which, m, pl.ds(zz * 8 + y * 2, 2)].reshape(2 * HITS, GROUP)
                        for zz in range(4)
                    ]
                    values = jnp.concatenate(rows, axis=0)
                else:
                    values = hits[which, m, pl.ds(z * 8, ROWS)].reshape(ROWS * HITS, GROUP)
                spread.append(dot(values.astype(F32).astype(BF16), choose))

            def lanes_of(values, col, half):
                parts = [
                    values[(half * 4 + q) * HITS : (half * 4 + q + 1) * HITS, col * TILE : (col + 1) * TILE]
                    for q in range(4)
                ]
                low = jnp.where(quarter == 0, parts[0], parts[1])
                high = jnp.where(quarter == 2, parts[2], parts[3])
                return jnp.where(quarter < 2, low, high)

            for col in range(COLS):
                tile_rows, sign_rows = [], []
                for half in range(2):
                    tile, block, sign = [lanes_of(values, col, half) for values in spread]
                    tile_rows.append(jnp.where(block == block_of_lane, tile, -1.0))
                    sign_rows.append(2.0 * sign - 1.0)
                tile_rows = jnp.concatenate(tile_rows, axis=1)
                sign_rows = jnp.concatenate(sign_rows, axis=1)
                total = jnp.zeros((BANK, 2 * TILE), F32)
                for h in range(HITS):
                    total += jnp.where(
                        tile_of_row == tile_rows[h : h + 1, :], sign_rows[h : h + 1, :], 0.0
                    )
                at = (m * COLS + col) * BANK
                count[kind, at : at + BANK, :] = total.astype(BF16)


def turn_bank(bank, bank_t):
    def turn(r, carry):
        bank_t[pl.ds(r, TILE, stride=BANK), :] = bank[r].astype(F32).T
        return carry

    lax.fori_loop(0, BANK, turn, 0, unroll=4)


def turn_rows(ins, left32, left, e, slot):
    for i in range(ROWS):
        left32[slot, pl.ds(i, TILE, stride=ROWS), :] = ins[e, i].astype(F32).T
    left[slot] = left32[slot].astype(BF16)


def spread_bank(bank_t, weights):
    lower = lax.broadcasted_iota(jnp.int32, (TILE, 2 * BANK), 1) < BANK

    def step(a, carry):
        tiles = bank_t[pl.ds(pl.multiple_of(a * BANK, BANK), BANK), :]
        turned = jnp.concatenate([tiles, tiles], axis=0).T
        weights[a, 0:TILE] = jnp.where(lower, turned, 0.0).astype(BF16)
        weights[a, TILE:] = jnp.where(lower, 0.0, turned).astype(BF16)
        return carry

    lax.fori_loop(0, TILE, step, 0, unroll=4)


def gradient(left, cots, grads, e, slot):
    rows = left[slot]
    for m in range(MATS):
        halves = []
        for col in range(0, COLS, 2):
            right = jnp.concatenate([cots[e, col, m], cots[e, col + 1, m]], axis=1)
            halves.append(dot(rows, right).reshape(TILE, ROWS, 2 * TILE))
        at = (slot * MATS + m) * 2 * ROWS
        grads[:, at : at + 2 * ROWS, :] = jnp.concatenate(halves, axis=1).astype(BF16)


def project(grads, weights, quads):
    def step(two, carry):
        outs = [dot(grads[two * 2 + u], weights[two * 2 + u]) for u in range(2)]
        at = pl.multiple_of(two * 2 * ROWS, 2 * ROWS)
        for slot in range(BATCH):
            for pair in range(PAIRS):
                src = (slot * PAIRS + pair) * ROWS
                both = jnp.concatenate([out[src : src + ROWS] for out in outs], axis=0)
                quads[slot, pl.ds(at, 2 * ROWS), pair * TILE : (pair + 1) * TILE] = both.astype(BF16)
        return carry

    lax.fori_loop(0, TILE // 2, step, 0, unroll=UNROLL)


def select(quads, count, picked, slot, kind):
    row_in_group = lax.rem(lax.broadcasted_iota(jnp.int32, (TILE * ROWS, TILE), 0), ROWS)
    lane_group = lax.broadcasted_iota(jnp.int32, (TILE * ROWS, TILE), 1) // BLOCKS
    sums = dot(quads[slot], count[kind])
    folded = jnp.where(row_in_group >= 4, sums[:, TILE:], sums[:, :TILE])
    picked[slot] = jnp.where(lane_group == lax.rem(row_in_group, 4), folded, 0.0)
    total = picked[slot, pl.ds(0, TILE, stride=ROWS), :]
    for i in range(1, ROWS):
        total += picked[slot, pl.ds(i, TILE, stride=ROWS), :]
    turned = total.T
    return turned[0:32] + turned[32:64] + turned[64:96] + turned[96:128]


def kernel(
    in_hbm, cot_hbm, bank_hbm, tiles_hbm, blocks_hbm, signs_hbm, test_hbm, out_ref,
    bank, bank_t, weights, hits, cots, ins, left32, left, grads, quads, picked, count, tests, tests_t,
    raw, sums_out, sums_in, done,
    load_sem, own_sem, j_send, j_recv, i_send, i_recv, p_send, p_recv, t_send, t_recv, ex_send, ex_recv,
):
    me = lax.axis_index("param")
    mx = lax.axis_index("ex")
    core = lax.rem(me, 2)
    y = lax.rem(me // 2, 4)
    z = me // 8

    def device(zz, yy, cc):
        return (zz * 4 + yy) * 2 + cc

    def along_y(distance):
        return device(z, lax.rem(y + distance, 4), core)

    def along_z(distance):
        return device(lax.rem(z + distance, 4), y, core)

    sibling = device(z, y, 1 - core)
    family, member = me // 4, lax.rem(me, 4)
    alone = member == mx

    barrier = pltpu.get_barrier_semaphore()

    def greet(**to):
        pl.semaphore_signal(barrier, inc=1, device_id=to, device_id_type=MESH)

    for d in (1, 3, 2):
        greet(param=along_y(d))
        greet(param=along_z(d))
    greet(param=sibling)
    for j in range(4):
        sender = family * 4 + j

        @pl.when(jnp.logical_or(sender != me, member != mx))
        def _(sender=sender):
            greet(param=sender, ex=member)

    loads = [
        pltpu.make_async_copy(tiles_hbm, hits.at[0], load_sem.at[0]),
        pltpu.make_async_copy(blocks_hbm, hits.at[1], load_sem.at[1]),
        pltpu.make_async_copy(signs_hbm, hits.at[2], load_sem.at[2]),
        pltpu.make_async_copy(bank_hbm, bank, load_sem.at[3]),
    ]
    for copy in loads:
        copy.start()
    own = []
    for kind in range(2):
        pair = pl.ds(2 * kind, 2)
        col_pos, row_pos = (y, z) if kind == 0 else (z, y)
        own.append(
            pltpu.make_async_copy(
                in_hbm.at[pair], ins.at[pair, row_pos * 2 + core], own_sem.at[kind]
            )
        )
        for e in (2 * kind, 2 * kind + 1):
            own.append(
                pltpu.make_async_copy(cot_hbm.at[:, e], cots.at[e, col_pos], own_sem.at[2 + e])
            )
    for copy in own:
        copy.start()

    for copy in loads[:3]:
        copy.wait()
    count_hits(hits, count, z, y, core)
    pl.semaphore_wait(barrier, 7 + jnp.where(alone, 3, 4))

    def send(src, dst, send_sem, recv_sem, **to):
        copy = pltpu.make_async_remote_copy(
            src_ref=src, dst_ref=dst, send_sem=send_sem, recv_sem=recv_sem, device_id=to, device_id_type=MESH
        )
        copy.start()
        return copy

    cols, rows, relays = {}, {}, {}
    early, late = ORDER[:BATCH], ORDER[BATCH:]

    def rings(e):
        return ((y, along_y), (z, along_z)) if e < 2 else ((z, along_z), (y, along_y))

    def send_tiles(batch):
        for e in batch:
            pos, to = rings(e)[1]
            place = ins.at[e, pos * 2 + core]
            for d in (2, 1, 3):
                rows[e, d] = send(in_hbm.at[e], place, i_send.at[e, d], i_recv.at[e, d], param=to(d))
            relays[e, 0] = send(in_hbm.at[e], place, p_send.at[e, 0], p_recv.at[e, 0], param=sibling)
        for e in batch:
            pos, to = rings(e)[0]
            for d in (2, 1, 3):
                cols[e, d] = send(
                    cot_hbm.at[:, e], cots.at[e, pos], j_send.at[e, d], j_recv.at[e, d], param=to(d)
                )

    def relay_rows(batch):
        for e in batch:
            pos = rings(e)[1][0]
            for d in (1, 3, 2):
                rows[e, d].wait_recv()
                place = ins.at[e, lax.rem(pos + 4 - d, 4) * 2 + core]
                relays[e, d] = send(place, place, p_send.at[e, d], p_recv.at[e, d], param=sibling)

    tests_out = []
    test_here = pltpu.make_async_copy(test_hbm, tests.at[member], t_recv.at[member])
    test_near = pltpu.make_async_remote_copy(
        src_ref=test_hbm,
        dst_ref=tests.at[member],
        send_sem=t_send.at[0],
        recv_sem=t_recv.at[member],
        device_id={"param": family * 4 + mx, "ex": mx},
        device_id_type=MESH,
    )

    def send_tests():
        for d in range(1, 4):
            tests_out.append(
                send(
                    test_hbm, tests.at[member], t_send.at[d], t_recv.at[member],
                    param=family * 4 + mx, ex=lax.rem(mx + d, 4),
                )
            )

        @pl.when(alone)
        def _():
            test_here.start()

        @pl.when(jnp.logical_not(alone))
        def _():
            test_near.start()

    def gradients(batch):
        for slot, e in enumerate(batch):
            for index in range(4):
                relays[e, index].wait_recv()
            turn_rows(ins, left32, left, e, slot)
        for slot, e in enumerate(batch):
            for d in (1, 3, 2):
                cols[e, d].wait_recv()
        if batch == late:
            send_tests()
        for slot, e in enumerate(batch):
            gradient(left, cots, grads, e, slot)

    def finish(batch):
        project(grads, weights, quads)
        for slot, e in enumerate(batch):
            raw[pl.ds(e, BLOCKS, stride=EX), :] = select(quads, count, picked, slot, e // 2)

    send_tiles(early)
    loads[3].wait()
    turn_bank(bank, bank_t)
    spread_bank(bank_t, weights)
    for copy in own:
        copy.wait()
    relay_rows(early)
    send_tiles(late)
    gradients(early)
    relay_rows(late)
    finish(early)
    gradients(late)
    finish(late)
    sums_out[...] = raw[...].astype(BF16).reshape(8, 4 * EX, TILE)

    others = sorted(
        [(dz, dy, dc) for dz in range(4) for dy in range(4) for dc in range(2)][1:],
        key=lambda d: -(min(d[0], 4 - d[0]) + min(d[1], 4 - d[1])),
    )

    def exchange(index, source, incoming, beside=None):
        for dz, dy, dc in others:
            to = device(lax.rem(z + dz, 4), lax.rem(y + dy, 4), lax.rem(core + dc, 2))
            send(source(to), incoming.at[me], ex_send.at[index], ex_recv.at[index], param=to)
        if beside is not None:
            beside()
        rest = incoming.at[pl.ds(0, GROUP - 1)]
        pltpu.make_async_copy(rest, rest, ex_recv.at[index]).wait()
        return pltpu.make_async_copy(rest, rest, ex_send.at[index])

    def drain():
        for j in range(4):
            pltpu.make_async_copy(tests.at[j], tests.at[j], t_recv.at[j]).wait()
            for half in range(2):
                piece = tests[j, half * TILE : (half + 1) * TILE].astype(F32).T
                tests_t[j, :, half * TILE : (half + 1) * TILE] = piece.astype(BF16)
        for copy in [*cols.values(), *rows.values(), *relays.values(), *tests_out]:
            copy.wait_send()

        @pl.when(jnp.logical_not(alone))
        def _():
            test_near.wait_send()

    sums_in[me] = sums_out[family]
    sums_sent = exchange(0, lambda to: sums_out.at[to // 4], sums_in, drain)
    features = jnp.sum(sums_in[...].astype(F32), axis=0) * SCALE
    high = features.astype(BF16)
    low = (features - high.astype(F32)).astype(BF16)
    scores = jnp.zeros((2 * EX, 256), F32)
    for j in range(4):
        both = jnp.concatenate([high[j * EX : (j + 1) * EX], low[j * EX : (j + 1) * EX]], axis=0)
        scores += dot(both, tests_t[j])
    done[me] = scores[:EX] + scores[EX:]
    scores_sent = exchange(1, lambda to: done.at[me], done, sums_sent.wait)
    for j in range(4):
        total = done[j]
        for other in range(1, 8):
            total += done[other * 4 + j]
        out_ref[:, j * 256 : (j + 1) * 256] = total
    scores_sent.wait()


def local(inputs, cotangents, jl_bank, jl_tiles, jl_blocks, jl_signs, test_features):
    turned = [jnp.transpose(a, (0, 1, 3, 2)) for a in (jl_tiles, jl_blocks, jl_signs)]
    anywhere = pl.BlockSpec(memory_space=pl.ANY)
    dma = pltpu.SemaphoreType.DMA
    return pl.pallas_call(
        kernel,
        out_shape=jax.ShapeDtypeStruct((EX, 1024), F32),
        in_specs=[anywhere] * 7,
        out_specs=pl.BlockSpec(memory_space=pltpu.VMEM),
        scratch_shapes=[
            pltpu.VMEM((BANK, TILE, TILE), BF16),
            pltpu.VMEM((TILE * BANK, TILE), F32),
            pltpu.VMEM((TILE, 2 * TILE, 2 * BANK), BF16),
            pltpu.VMEM((3, MATS, GROUP, HITS, GROUP), jnp.int32),
            pltpu.VMEM((EX, COLS, MATS, TOK, TILE), BF16),
            pltpu.VMEM((EX, ROWS, TOK, TILE), BF16),
            pltpu.VMEM((BATCH, TILE * ROWS, TOK), F32),
            pltpu.VMEM((BATCH, TILE * ROWS, TOK), BF16),
            pltpu.VMEM((TILE, BATCH * PAIRS * ROWS, 2 * TILE), BF16),
            pltpu.VMEM((BATCH, TILE * ROWS, PAIRS * TILE), BF16),
            pltpu.VMEM((BATCH, TILE * ROWS, TILE), F32),
            pltpu.VMEM((2, MATS * COLS * BANK, 2 * TILE), BF16),
            pltpu.VMEM((4, 256, TILE), BF16),
            pltpu.VMEM((4, TILE, 256), BF16),
            pltpu.VMEM((BLOCKS * EX, TILE), F32),
            pltpu.VMEM((8, 4 * EX, TILE), BF16),
            pltpu.VMEM((GROUP, 4 * EX, TILE), BF16),
            pltpu.VMEM((GROUP, EX, 256), F32),
            dma((4,)),
            dma((2 + EX,)),
            dma((EX, 4)),
            dma((EX, 4)),
            dma((EX, 4)),
            dma((EX, 4)),
            dma((EX, 4)),
            dma((EX, 4)),
            dma((4,)),
            dma((4,)),
            dma((2,)),
            dma((2,)),
        ],
        compiler_params=pltpu.CompilerParams(
            collective_id=0, has_side_effects=True, vmem_limit_bytes=56 * 1024 * 1024
        ),
        cost_estimate=pl.CostEstimate(flops=9_000_000_000, bytes_accessed=8_000_000, transcendentals=0),
    )(inputs, cotangents, jl_bank, *turned, test_features)


def solution(mesh):
    placed = (
        P("ex", None, "param"),
        P(None, "ex", None, "param"),
        P(),
        P(),
        P(),
        P(),
        P("ex", "param"),
    )
    return jax.shard_map(
        local, mesh=mesh, in_specs=placed, out_specs=P("ex", None), check_vma=False
    )
```

```python
import functools
import math

import jax
import jax.numpy as jnp
from jax import lax
from jax.experimental import pallas as pl
from jax.experimental.pallas import tpu as pltpu
from jax.sharding import PartitionSpec as P

D = 4096
K = 4096
TILE = 128
HITS = 8
MATS = 3
TOK = 128
BANK = 64
BLOCKS = 32
EX = 4
ROWS = 8
COLS = 4
PAIRS = MATS * COLS // 2
GROUP = 32
BATCH = 2
UNROLL = 32
MESH = pl.DeviceIdType.MESH
F32 = jnp.float32
BF16 = jnp.bfloat16
SCALE = 1.0 / (math.sqrt(TOK * MATS * HITS * D * D / (TILE * K)) * math.sqrt(K))
ORDER = (0, 2, 1, 3)


def dot(a, b):
    return lax.dot_general(a, b, (((1,), (0,)), ((), ())), preferred_element_type=F32)


def count_hits(hits, count, z, y, core):
    lane = lax.broadcasted_iota(jnp.int32, (HITS, TILE), 1)
    block_of_lane = lax.rem(lane, BLOCKS).astype(F32)
    quarter = lane // BLOCKS
    tile_of_row = lax.broadcasted_iota(jnp.int32, (BANK, 2 * TILE), 0).astype(F32)
    for kind in range(2):
        first, step = (z * 8 + core, 2) if kind == 0 else (y * 2 + core, 8)
        source = lax.broadcasted_iota(jnp.int32, (GROUP, COLS * TILE), 0)
        column = lax.broadcasted_iota(jnp.int32, (GROUP, COLS * TILE), 1) // TILE
        choose = jnp.where(source == first + step * column, 1.0, 0.0).astype(BF16)
        for m in range(MATS):
            spread = []
            for which in range(3):
                if kind == 0:
                    rows = [
                        hits[which, m, pl.ds(zz * 8 + y * 2, 2)].reshape(2 * HITS, GROUP)
                        for zz in range(4)
                    ]
                    values = jnp.concatenate(rows, axis=0)
                else:
                    values = hits[which, m, pl.ds(z * 8, ROWS)].reshape(ROWS * HITS, GROUP)
                spread.append(dot(values.astype(F32).astype(BF16), choose))

            def lanes_of(values, col, half):
                parts = [
                    values[(half * 4 + q) * HITS : (half * 4 + q + 1) * HITS, col * TILE : (col + 1) * TILE]
                    for q in range(4)
                ]
                low = jnp.where(quarter == 0, parts[0], parts[1])
                high = jnp.where(quarter == 2, parts[2], parts[3])
                return jnp.where(quarter < 2, low, high)

            for col in range(COLS):
                tile_rows, sign_rows = [], []
                for half in range(2):
                    tile, block, sign = [lanes_of(values, col, half) for values in spread]
                    tile_rows.append(jnp.where(block == block_of_lane, tile, -1.0))
                    sign_rows.append(2.0 * sign - 1.0)
                tile_rows = jnp.concatenate(tile_rows, axis=1)
                sign_rows = jnp.concatenate(sign_rows, axis=1)
                total = jnp.zeros((BANK, 2 * TILE), F32)
                for h in range(HITS):
                    total += jnp.where(
                        tile_of_row == tile_rows[h : h + 1, :], sign_rows[h : h + 1, :], 0.0
                    )
                at = (m * COLS + col) * BANK
                count[kind, at : at + BANK, :] = total.astype(BF16)


def turn_bank(bank, bank_t):
    def turn(r, carry):
        bank_t[pl.ds(r, TILE, stride=BANK), :] = bank[r].astype(F32).T
        return carry

    lax.fori_loop(0, BANK, turn, 0, unroll=4)


def turn_rows(ins, left32, left, e, slot):
    for i in range(ROWS):
        left32[slot, pl.ds(i, TILE, stride=ROWS), :] = ins[e, i].astype(F32).T
    left[slot] = left32[slot].astype(BF16)


def spread_bank(bank_t, weights):
    lower = lax.broadcasted_iota(jnp.int32, (TILE, 2 * BANK), 1) < BANK

    def step(a, carry):
        tiles = bank_t[pl.ds(pl.multiple_of(a * BANK, BANK), BANK), :]
        turned = jnp.concatenate([tiles, tiles], axis=0).T
        weights[a, 0:TILE] = jnp.where(lower, turned, 0.0).astype(BF16)
        weights[a, TILE:] = jnp.where(lower, 0.0, turned).astype(BF16)
        return carry

    lax.fori_loop(0, TILE, step, 0, unroll=4)


def gradient(left, cots, grads, e, slot):
    rows = left[slot]
    for m in range(MATS):
        halves = []
        for col in range(0, COLS, 2):
            right = jnp.concatenate([cots[e, col, m], cots[e, col + 1, m]], axis=1)
            halves.append(dot(rows, right).reshape(TILE, ROWS, 2 * TILE))
        at = (slot * MATS + m) * 2 * ROWS
        grads[:, at : at + 2 * ROWS, :] = jnp.concatenate(halves, axis=1).astype(BF16)


def project(grads, weights, quads):
    def step(two, carry):
        outs = [dot(grads[two * 2 + u], weights[two * 2 + u]) for u in range(2)]
        at = pl.multiple_of(two * 2 * ROWS, 2 * ROWS)
        for slot in range(BATCH):
            for pair in range(PAIRS):
                src = (slot * PAIRS + pair) * ROWS
                both = jnp.concatenate([out[src : src + ROWS] for out in outs], axis=0)
                quads[slot, pl.ds(at, 2 * ROWS), pair * TILE : (pair + 1) * TILE] = both.astype(BF16)
        return carry

    lax.fori_loop(0, TILE // 2, step, 0, unroll=UNROLL)


def select(quads, count, picked, slot, kind):
    row_in_group = lax.rem(lax.broadcasted_iota(jnp.int32, (TILE * ROWS, TILE), 0), ROWS)
    lane_group = lax.broadcasted_iota(jnp.int32, (TILE * ROWS, TILE), 1) // BLOCKS
    sums = dot(quads[slot], count[kind])
    folded = jnp.where(row_in_group >= 4, sums[:, TILE:], sums[:, :TILE])
    picked[slot] = jnp.where(lane_group == lax.rem(row_in_group, 4), folded, 0.0)
    total = picked[slot, pl.ds(0, TILE, stride=ROWS), :]
    for i in range(1, ROWS):
        total += picked[slot, pl.ds(i, TILE, stride=ROWS), :]
    turned = total.T
    return turned[0:32] + turned[32:64] + turned[64:96] + turned[96:128]


def kernel(
    in_hbm, cot_hbm, bank_hbm, tiles_hbm, blocks_hbm, signs_hbm, test_hbm, out_ref,
    bank, bank_t, weights, hits, cots, ins, left32, left, grads, quads, picked, count, tests, tests_t,
    raw, sums_out, sums_in, done,
    load_sem, own_sem, j_send, j_recv, i_send, i_recv, p_send, p_recv, t_send, t_recv, ex_send, ex_recv,
):
    me = lax.axis_index("param")
    mx = lax.axis_index("ex")
    core = lax.rem(me, 2)
    y = lax.rem(me // 2, 4)
    z = me // 8

    def device(zz, yy, cc):
        return (zz * 4 + yy) * 2 + cc

    def along_y(distance):
        return device(z, lax.rem(y + distance, 4), core)

    def along_z(distance):
        return device(lax.rem(z + distance, 4), y, core)

    sibling = device(z, y, 1 - core)
    family, member = me // 4, lax.rem(me, 4)
    alone = member == mx

    barrier = pltpu.get_barrier_semaphore()

    def greet(**to):
        pl.semaphore_signal(barrier, inc=1, device_id=to, device_id_type=MESH)

    for j in range(4):
        sender = family * 4 + j

        @pl.when(jnp.logical_or(sender != me, member != mx))
        def _(sender=sender):
            greet(param=sender, ex=member)

    for d in (2, 1, 3):
        greet(param=along_y(d))
        greet(param=along_z(d))
    greet(param=sibling)
    loads = [
        pltpu.make_async_copy(tiles_hbm, hits.at[0], load_sem.at[0]),
        pltpu.make_async_copy(blocks_hbm, hits.at[1], load_sem.at[1]),
        pltpu.make_async_copy(signs_hbm, hits.at[2], load_sem.at[2]),
        pltpu.make_async_copy(bank_hbm, bank, load_sem.at[3]),
    ]
    for copy in loads:
        copy.start()
    own = []
    for kind in range(2):
        pair = pl.ds(2 * kind, 2)
        col_pos, row_pos = (y, z) if kind == 0 else (z, y)
        own.append(
            pltpu.make_async_copy(
                in_hbm.at[pair], ins.at[pair, row_pos * 2 + core], own_sem.at[kind]
            )
        )
        for e in (2 * kind, 2 * kind + 1):
            own.append(
                pltpu.make_async_copy(cot_hbm.at[:, e], cots.at[e, col_pos], own_sem.at[2 + e])
            )
    for copy in own:
        copy.start()

    pl.semaphore_wait(barrier, 7 + jnp.where(alone, 3, 4))

    def send(src, dst, send_sem, recv_sem, **to):
        copy = pltpu.make_async_remote_copy(
            src_ref=src, dst_ref=dst, send_sem=send_sem, recv_sem=recv_sem, device_id=to, device_id_type=MESH
        )
        copy.start()
        return copy

    cols, rows, relays = {}, {}, {}
    early, late = ORDER[:BATCH], ORDER[BATCH:]

    def rings(e):
        return ((y, along_y), (z, along_z)) if e < 2 else ((z, along_z), (y, along_y))

    def send_tiles(batch):
        for e in batch:
            pos, to = rings(e)[1]
            place = ins.at[e, pos * 2 + core]
            for d in (2, 1, 3):
                rows[e, d] = send(in_hbm.at[e], place, i_send.at[e, d], i_recv.at[e, d], param=to(d))
            relays[e, 0] = send(in_hbm.at[e], place, p_send.at[e, 0], p_recv.at[e, 0], param=sibling)
        for e in batch:
            pos, to = rings(e)[0]
            for d in (2, 1, 3):
                cols[e, d] = send(
                    cot_hbm.at[:, e], cots.at[e, pos], j_send.at[e, d], j_recv.at[e, d], param=to(d)
                )

    def relay_rows(batch):
        for e in batch:
            pos = rings(e)[1][0]
            for d in (1, 3, 2):
                rows[e, d].wait_recv()
                place = ins.at[e, lax.rem(pos + 4 - d, 4) * 2 + core]
                relays[e, d] = send(place, place, p_send.at[e, d], p_recv.at[e, d], param=sibling)

    tests_out = []
    test_here = pltpu.make_async_copy(test_hbm, tests.at[member], t_recv.at[member])
    test_near = pltpu.make_async_remote_copy(
        src_ref=test_hbm,
        dst_ref=tests.at[member],
        send_sem=t_send.at[0],
        recv_sem=t_recv.at[member],
        device_id={"param": family * 4 + mx, "ex": mx},
        device_id_type=MESH,
    )

    def send_tests():
        for d in range(1, 4):
            tests_out.append(
                send(
                    test_hbm, tests.at[member], t_send.at[d], t_recv.at[member],
                    param=family * 4 + mx, ex=lax.rem(mx + d, 4),
                )
            )

        @pl.when(alone)
        def _():
            test_here.start()

        @pl.when(jnp.logical_not(alone))
        def _():
            test_near.start()

    def gradients(batch):
        for slot, e in enumerate(batch):
            for index in range(4):
                relays[e, index].wait_recv()
            turn_rows(ins, left32, left, e, slot)
        for slot, e in enumerate(batch):
            for d in (1, 3, 2):
                cols[e, d].wait_recv()
        if batch == late:
            send_tests()
        for slot, e in enumerate(batch):
            gradient(left, cots, grads, e, slot)

    def finish(batch):
        project(grads, weights, quads)
        for slot, e in enumerate(batch):
            raw[pl.ds(e, BLOCKS, stride=EX), :] = select(quads, count, picked, slot, e // 2)

    send_tiles(early)

    for copy in loads[:3]:
        copy.wait()
    count_hits(hits, count, z, y, core)
    loads[3].wait()
    turn_bank(bank, bank_t)
    for copy in own:
        copy.wait()
    relay_rows(early)
    send_tiles(late)
    spread_bank(bank_t, weights)
    gradients(early)
    relay_rows(late)
    finish(early)
    gradients(late)
    finish(late)
    sums_out[...] = raw[...].astype(BF16).reshape(8, 4 * EX, TILE)

    others = sorted(
        [(dz, dy, dc) for dz in range(4) for dy in range(4) for dc in range(2)][1:],
        key=lambda d: -(min(d[0], 4 - d[0]) + min(d[1], 4 - d[1])),
    )

    def exchange(index, source, incoming, beside=None):
        for dz, dy, dc in others:
            to = device(lax.rem(z + dz, 4), lax.rem(y + dy, 4), lax.rem(core + dc, 2))
            send(source(to), incoming.at[me], ex_send.at[index], ex_recv.at[index], param=to)
        if beside is not None:
            beside()
        rest = incoming.at[pl.ds(0, GROUP - 1)]
        pltpu.make_async_copy(rest, rest, ex_recv.at[index]).wait()
        return pltpu.make_async_copy(rest, rest, ex_send.at[index])

    def drain():
        for j in range(4):
            pltpu.make_async_copy(tests.at[j], tests.at[j], t_recv.at[j]).wait()
            for half in range(2):
                piece = tests[j, half * TILE : (half + 1) * TILE].astype(F32).T
                tests_t[j, :, half * TILE : (half + 1) * TILE] = piece.astype(BF16)
        for copy in [*cols.values(), *rows.values(), *relays.values(), *tests_out]:
            copy.wait_send()

        @pl.when(jnp.logical_not(alone))
        def _():
            test_near.wait_send()

    sums_in[me] = sums_out[family]
    sums_sent = exchange(0, lambda to: sums_out.at[to // 4], sums_in, drain)
    features = jnp.sum(sums_in[...].astype(F32), axis=0) * SCALE
    high = features.astype(BF16)
    low = (features - high.astype(F32)).astype(BF16)
    scores = jnp.zeros((2 * EX, 256), F32)
    for j in range(4):
        both = jnp.concatenate([high[j * EX : (j + 1) * EX], low[j * EX : (j + 1) * EX]], axis=0)
        scores += dot(both, tests_t[j])
    done[me] = scores[:EX] + scores[EX:]
    scores_sent = exchange(1, lambda to: done.at[me], done, sums_sent.wait)
    for j in range(4):
        total = done[j]
        for other in range(1, 8):
            total += done[other * 4 + j]
        out_ref[:, j * 256 : (j + 1) * 256] = total
    scores_sent.wait()


def local(inputs, cotangents, jl_bank, jl_tiles, jl_blocks, jl_signs, test_features):
    turned = [jnp.transpose(a, (0, 1, 3, 2)) for a in (jl_tiles, jl_blocks, jl_signs)]
    anywhere = pl.BlockSpec(memory_space=pl.ANY)
    dma = pltpu.SemaphoreType.DMA
    return pl.pallas_call(
        kernel,
        out_shape=jax.ShapeDtypeStruct((EX, 1024), F32),
        in_specs=[anywhere] * 7,
        out_specs=pl.BlockSpec(memory_space=pltpu.VMEM),
        scratch_shapes=[
            pltpu.VMEM((BANK, TILE, TILE), BF16),
            pltpu.VMEM((TILE * BANK, TILE), F32),
            pltpu.VMEM((TILE, 2 * TILE, 2 * BANK), BF16),
            pltpu.VMEM((3, MATS, GROUP, HITS, GROUP), jnp.int32),
            pltpu.VMEM((EX, COLS, MATS, TOK, TILE), BF16),
            pltpu.VMEM((EX, ROWS, TOK, TILE), BF16),
            pltpu.VMEM((BATCH, TILE * ROWS, TOK), F32),
            pltpu.VMEM((BATCH, TILE * ROWS, TOK), BF16),
            pltpu.VMEM((TILE, BATCH * PAIRS * ROWS, 2 * TILE), BF16),
            pltpu.VMEM((BATCH, TILE * ROWS, PAIRS * TILE), BF16),
            pltpu.VMEM((BATCH, TILE * ROWS, TILE), F32),
            pltpu.VMEM((2, MATS * COLS * BANK, 2 * TILE), BF16),
            pltpu.VMEM((4, 256, TILE), BF16),
            pltpu.VMEM((4, TILE, 256), BF16),
            pltpu.VMEM((BLOCKS * EX, TILE), F32),
            pltpu.VMEM((8, 4 * EX, TILE), BF16),
            pltpu.VMEM((GROUP, 4 * EX, TILE), BF16),
            pltpu.VMEM((GROUP, EX, 256), F32),
            dma((4,)),
            dma((2 + EX,)),
            dma((EX, 4)),
            dma((EX, 4)),
            dma((EX, 4)),
            dma((EX, 4)),
            dma((EX, 4)),
            dma((EX, 4)),
            dma((4,)),
            dma((4,)),
            dma((2,)),
            dma((2,)),
        ],
        compiler_params=pltpu.CompilerParams(
            collective_id=0, has_side_effects=True, vmem_limit_bytes=56 * 1024 * 1024
        ),
        cost_estimate=pl.CostEstimate(flops=9_000_000_000, bytes_accessed=8_000_000, transcendentals=0),
    )(inputs, cotangents, jl_bank, *turned, test_features)


def solution(mesh):
    placed = (
        P("ex", None, "param"),
        P(None, "ex", None, "param"),
        P(),
        P(),
        P(),
        P(),
        P("ex", "param"),
    )
    return jax.shard_map(
        local, mesh=mesh, in_specs=placed, out_specs=P("ex", None), check_vma=False
    )
```

```python
import functools
import math

import jax
import jax.numpy as jnp
from jax import lax
from jax.experimental import pallas as pl
from jax.experimental.pallas import tpu as pltpu
from jax.sharding import PartitionSpec as P

D = 4096
K = 4096
TILE = 128
HITS = 8
MATS = 3
TOK = 128
BANK = 64
BLOCKS = 32
EX = 4
ROWS = 8
COLS = 4
PAIRS = MATS * COLS // 2
GROUP = 32
BATCH = 2
UNROLL = 64
MESH = pl.DeviceIdType.MESH
F32 = jnp.float32
BF16 = jnp.bfloat16
SCALE = 1.0 / (math.sqrt(TOK * MATS * HITS * D * D / (TILE * K)) * math.sqrt(K))
ORDER = (0, 2, 1, 3)


def dot(a, b):
    return lax.dot_general(a, b, (((1,), (0,)), ((), ())), preferred_element_type=F32)


def count_hits(hits, count, z, y, core):
    lane = lax.broadcasted_iota(jnp.int32, (HITS, TILE), 1)
    block_of_lane = lax.rem(lane, BLOCKS).astype(F32)
    quarter = lane // BLOCKS
    tile_of_row = lax.broadcasted_iota(jnp.int32, (BANK, 2 * TILE), 0).astype(F32)
    for kind in range(2):
        first, step = (z * 8 + core, 2) if kind == 0 else (y * 2 + core, 8)
        source = lax.broadcasted_iota(jnp.int32, (GROUP, COLS * TILE), 0)
        column = lax.broadcasted_iota(jnp.int32, (GROUP, COLS * TILE), 1) // TILE
        choose = jnp.where(source == first + step * column, 1.0, 0.0).astype(BF16)
        for m in range(MATS):
            spread = []
            for which in range(3):
                if kind == 0:
                    rows = [
                        hits[which, m, pl.ds(zz * 8 + y * 2, 2)].reshape(2 * HITS, GROUP)
                        for zz in range(4)
                    ]
                    values = jnp.concatenate(rows, axis=0)
                else:
                    values = hits[which, m, pl.ds(z * 8, ROWS)].reshape(ROWS * HITS, GROUP)
                spread.append(dot(values.astype(F32).astype(BF16), choose))

            def lanes_of(values, col, half):
                parts = [
                    values[(half * 4 + q) * HITS : (half * 4 + q + 1) * HITS, col * TILE : (col + 1) * TILE]
                    for q in range(4)
                ]
                low = jnp.where(quarter == 0, parts[0], parts[1])
                high = jnp.where(quarter == 2, parts[2], parts[3])
                return jnp.where(quarter < 2, low, high)

            for col in range(COLS):
                tile_rows, sign_rows = [], []
                for half in range(2):
                    tile, block, sign = [lanes_of(values, col, half) for values in spread]
                    tile_rows.append(jnp.where(block == block_of_lane, tile, -1.0))
                    sign_rows.append(2.0 * sign - 1.0)
                tile_rows = jnp.concatenate(tile_rows, axis=1)
                sign_rows = jnp.concatenate(sign_rows, axis=1)
                total = jnp.zeros((BANK, 2 * TILE), F32)
                for h in range(HITS):
                    total += jnp.where(
                        tile_of_row == tile_rows[h : h + 1, :], sign_rows[h : h + 1, :], 0.0
                    )
                at = (m * COLS + col) * BANK
                count[kind, at : at + BANK, :] = total.astype(BF16)


def turn_bank(bank, bank_t):
    def turn(r, carry):
        bank_t[pl.ds(r, TILE, stride=BANK), :] = bank[r].astype(F32).T
        return carry

    lax.fori_loop(0, BANK, turn, 0, unroll=16)


def turn_rows(ins, left32, left, e, slot):
    for i in range(ROWS):
        left32[slot, pl.ds(i, TILE, stride=ROWS), :] = ins[e, i].astype(F32).T
    left[slot] = left32[slot].astype(BF16)


def spread_bank(bank_t, weights):
    lower = lax.broadcasted_iota(jnp.int32, (TILE, 2 * BANK), 1) < BANK

    def step(a, carry):
        tiles = bank_t[pl.ds(pl.multiple_of(a * BANK, BANK), BANK), :]
        turned = jnp.concatenate([tiles, tiles], axis=0).T
        weights[a, 0:TILE] = jnp.where(lower, turned, 0.0).astype(BF16)
        weights[a, TILE:] = jnp.where(lower, 0.0, turned).astype(BF16)
        return carry

    lax.fori_loop(0, TILE, step, 0, unroll=16)


def gradient(left, cots, grads, e, slot):
    rows = left[slot]
    for m in range(MATS):
        halves = []
        for col in range(0, COLS, 2):
            right = jnp.concatenate([cots[e, col, m], cots[e, col + 1, m]], axis=1)
            halves.append(dot(rows, right).reshape(TILE, ROWS, 2 * TILE))
        at = (slot * MATS + m) * 2 * ROWS
        grads[:, at : at + 2 * ROWS, :] = jnp.concatenate(halves, axis=1).astype(BF16)


def project(grads, weights, quads):
    def step(two, carry):
        outs = [dot(grads[two * 2 + u], weights[two * 2 + u]) for u in range(2)]
        at = pl.multiple_of(two * 2 * ROWS, 2 * ROWS)
        for slot in range(BATCH):
            for pair in range(PAIRS):
                src = (slot * PAIRS + pair) * ROWS
                both = jnp.concatenate([out[src : src + ROWS] for out in outs], axis=0)
                quads[slot, pl.ds(at, 2 * ROWS), pair * TILE : (pair + 1) * TILE] = both.astype(BF16)
        return carry

    lax.fori_loop(0, TILE // 2, step, 0, unroll=UNROLL)


def select(quads, count, picked, slot, kind):
    row_in_group = lax.rem(lax.broadcasted_iota(jnp.int32, (TILE * ROWS, TILE), 0), ROWS)
    lane_group = lax.broadcasted_iota(jnp.int32, (TILE * ROWS, TILE), 1) // BLOCKS
    sums = dot(quads[slot], count[kind])
    folded = jnp.where(row_in_group >= 4, sums[:, TILE:], sums[:, :TILE])
    picked[slot] = jnp.where(lane_group == lax.rem(row_in_group, 4), folded, 0.0)
    total = picked[slot, pl.ds(0, TILE, stride=ROWS), :]
    for i in range(1, ROWS):
        total += picked[slot, pl.ds(i, TILE, stride=ROWS), :]
    turned = total.T
    return turned[0:32] + turned[32:64] + turned[64:96] + turned[96:128]


def kernel(
    in_hbm, cot_hbm, bank_hbm, tiles_hbm, blocks_hbm, signs_hbm, test_hbm, out_ref,
    bank, bank_t, weights, hits, cots, ins, left32, left, grads, quads, picked, count, tests, tests_t,
    raw, sums_out, sums_in, done,
    load_sem, own_sem, j_send, j_recv, i_send, i_recv, p_send, p_recv, t_send, t_recv, ex_send, ex_recv,
):
    me = lax.axis_index("param")
    mx = lax.axis_index("ex")
    core = lax.rem(me, 2)
    y = lax.rem(me // 2, 4)
    z = me // 8

    def device(zz, yy, cc):
        return (zz * 4 + yy) * 2 + cc

    def along_y(distance):
        return device(z, lax.rem(y + distance, 4), core)

    def along_z(distance):
        return device(lax.rem(z + distance, 4), y, core)

    sibling = device(z, y, 1 - core)
    family, member = me // 4, lax.rem(me, 4)
    alone = member == mx

    barrier = pltpu.get_barrier_semaphore()

    def greet(**to):
        pl.semaphore_signal(barrier, inc=1, device_id=to, device_id_type=MESH)

    for j in range(4):
        sender = family * 4 + j

        @pl.when(jnp.logical_or(sender != me, member != mx))
        def _(sender=sender):
            greet(param=sender, ex=member)

    for d in (2, 1, 3):
        greet(param=along_y(d))
        greet(param=along_z(d))
    greet(param=sibling)
    loads = [
        pltpu.make_async_copy(tiles_hbm, hits.at[0], load_sem.at[0]),
        pltpu.make_async_copy(blocks_hbm, hits.at[1], load_sem.at[1]),
        pltpu.make_async_copy(signs_hbm, hits.at[2], load_sem.at[2]),
        pltpu.make_async_copy(bank_hbm, bank, load_sem.at[3]),
    ]
    for copy in loads:
        copy.start()
    own = []
    for kind in range(2):
        pair = pl.ds(2 * kind, 2)
        col_pos, row_pos = (y, z) if kind == 0 else (z, y)
        own.append(
            pltpu.make_async_copy(
                in_hbm.at[pair], ins.at[pair, row_pos * 2 + core], own_sem.at[kind]
            )
        )
        for e in (2 * kind, 2 * kind + 1):
            own.append(
                pltpu.make_async_copy(cot_hbm.at[:, e], cots.at[e, col_pos], own_sem.at[2 + e])
            )
    for copy in own:
        copy.start()

    pl.semaphore_wait(barrier, 7 + jnp.where(alone, 3, 4))

    def send(src, dst, send_sem, recv_sem, **to):
        copy = pltpu.make_async_remote_copy(
            src_ref=src, dst_ref=dst, send_sem=send_sem, recv_sem=recv_sem, device_id=to, device_id_type=MESH
        )
        copy.start()
        return copy

    cols, rows, relays = {}, {}, {}
    early, late = ORDER[:BATCH], ORDER[BATCH:]

    def rings(e):
        return ((y, along_y), (z, along_z)) if e < 2 else ((z, along_z), (y, along_y))

    def send_tiles(batch):
        for e in batch:
            pos, to = rings(e)[1]
            place = ins.at[e, pos * 2 + core]
            for d in (2, 1, 3):
                rows[e, d] = send(in_hbm.at[e], place, i_send.at[e, d], i_recv.at[e, d], param=to(d))
            relays[e, 0] = send(in_hbm.at[e], place, p_send.at[e, 0], p_recv.at[e, 0], param=sibling)
        for e in batch:
            pos, to = rings(e)[0]
            for d in (2, 1, 3):
                cols[e, d] = send(
                    cot_hbm.at[:, e], cots.at[e, pos], j_send.at[e, d], j_recv.at[e, d], param=to(d)
                )

    def relay_rows(batch):
        for e in batch:
            pos = rings(e)[1][0]
            for d in (1, 3, 2):
                rows[e, d].wait_recv()
                place = ins.at[e, lax.rem(pos + 4 - d, 4) * 2 + core]
                relays[e, d] = send(place, place, p_send.at[e, d], p_recv.at[e, d], param=sibling)

    tests_out = []
    test_here = pltpu.make_async_copy(test_hbm, tests.at[member], t_recv.at[member])
    test_near = pltpu.make_async_remote_copy(
        src_ref=test_hbm,
        dst_ref=tests.at[member],
        send_sem=t_send.at[0],
        recv_sem=t_recv.at[member],
        device_id={"param": family * 4 + mx, "ex": mx},
        device_id_type=MESH,
    )

    def send_tests():
        for d in range(1, 4):
            tests_out.append(
                send(
                    test_hbm, tests.at[member], t_send.at[d], t_recv.at[member],
                    param=family * 4 + mx, ex=lax.rem(mx + d, 4),
                )
            )

        @pl.when(alone)
        def _():
            test_here.start()

        @pl.when(jnp.logical_not(alone))
        def _():
            test_near.start()

    def gradients(batch):
        for slot, e in enumerate(batch):
            for index in range(4):
                relays[e, index].wait_recv()
            turn_rows(ins, left32, left, e, slot)
        for slot, e in enumerate(batch):
            for d in (1, 3, 2):
                cols[e, d].wait_recv()
        if batch == late:
            send_tests()
        for slot, e in enumerate(batch):
            gradient(left, cots, grads, e, slot)

    def finish(batch):
        project(grads, weights, quads)
        for slot, e in enumerate(batch):
            raw[pl.ds(e, BLOCKS, stride=EX), :] = select(quads, count, picked, slot, e // 2)

    send_tiles(early)

    for copy in loads[:3]:
        copy.wait()
    count_hits(hits, count, z, y, core)
    loads[3].wait()
    turn_bank(bank, bank_t)
    for copy in own:
        copy.wait()
    relay_rows(early)
    send_tiles(late)
    spread_bank(bank_t, weights)
    gradients(early)
    relay_rows(late)
    finish(early)
    gradients(late)
    finish(late)
    sums_out[...] = raw[...].astype(BF16).reshape(8, 4 * EX, TILE)

    others = sorted(
        [(dz, dy, dc) for dz in range(4) for dy in range(4) for dc in range(2)][1:],
        key=lambda d: -(min(d[0], 4 - d[0]) + min(d[1], 4 - d[1])),
    )

    def exchange(index, source, incoming, beside=None):
        for dz, dy, dc in others:
            to = device(lax.rem(z + dz, 4), lax.rem(y + dy, 4), lax.rem(core + dc, 2))
            send(source(to), incoming.at[me], ex_send.at[index], ex_recv.at[index], param=to)
        if beside is not None:
            beside()
        rest = incoming.at[pl.ds(0, GROUP - 1)]
        pltpu.make_async_copy(rest, rest, ex_recv.at[index]).wait()
        return pltpu.make_async_copy(rest, rest, ex_send.at[index])

    def drain():
        for j in range(4):
            pltpu.make_async_copy(tests.at[j], tests.at[j], t_recv.at[j]).wait()
            for half in range(2):
                piece = tests[j, half * TILE : (half + 1) * TILE].astype(F32).T
                tests_t[j, :, half * TILE : (half + 1) * TILE] = piece.astype(BF16)
        for copy in [*cols.values(), *rows.values(), *relays.values(), *tests_out]:
            copy.wait_send()

        @pl.when(jnp.logical_not(alone))
        def _():
            test_near.wait_send()

    sums_in[me] = sums_out[family]
    sums_sent = exchange(0, lambda to: sums_out.at[to // 4], sums_in, drain)
    features = jnp.sum(sums_in[...].astype(F32), axis=0) * SCALE
    high = features.astype(BF16)
    low = (features - high.astype(F32)).astype(BF16)
    scores = jnp.zeros((2 * EX, 256), F32)
    for j in range(4):
        both = jnp.concatenate([high[j * EX : (j + 1) * EX], low[j * EX : (j + 1) * EX]], axis=0)
        scores += dot(both, tests_t[j])
    done[me] = scores[:EX] + scores[EX:]
    scores_sent = exchange(1, lambda to: done.at[me], done, sums_sent.wait)
    for j in range(4):
        total = done[j]
        for other in range(1, 8):
            total += done[other * 4 + j]
        out_ref[:, j * 256 : (j + 1) * 256] = total
    scores_sent.wait()


def local(inputs, cotangents, jl_bank, jl_tiles, jl_blocks, jl_signs, test_features):
    turned = [jnp.transpose(a, (0, 1, 3, 2)) for a in (jl_tiles, jl_blocks, jl_signs)]
    anywhere = pl.BlockSpec(memory_space=pl.ANY)
    dma = pltpu.SemaphoreType.DMA
    return pl.pallas_call(
        kernel,
        out_shape=jax.ShapeDtypeStruct((EX, 1024), F32),
        in_specs=[anywhere] * 7,
        out_specs=pl.BlockSpec(memory_space=pltpu.VMEM),
        scratch_shapes=[
            pltpu.VMEM((BANK, TILE, TILE), BF16),
            pltpu.VMEM((TILE * BANK, TILE), F32),
            pltpu.VMEM((TILE, 2 * TILE, 2 * BANK), BF16),
            pltpu.VMEM((3, MATS, GROUP, HITS, GROUP), jnp.int32),
            pltpu.VMEM((EX, COLS, MATS, TOK, TILE), BF16),
            pltpu.VMEM((EX, ROWS, TOK, TILE), BF16),
            pltpu.VMEM((BATCH, TILE * ROWS, TOK), F32),
            pltpu.VMEM((BATCH, TILE * ROWS, TOK), BF16),
            pltpu.VMEM((TILE, BATCH * PAIRS * ROWS, 2 * TILE), BF16),
            pltpu.VMEM((BATCH, TILE * ROWS, PAIRS * TILE), BF16),
            pltpu.VMEM((BATCH, TILE * ROWS, TILE), F32),
            pltpu.VMEM((2, MATS * COLS * BANK, 2 * TILE), BF16),
            pltpu.VMEM((4, 256, TILE), BF16),
            pltpu.VMEM((4, TILE, 256), BF16),
            pltpu.VMEM((BLOCKS * EX, TILE), F32),
            pltpu.VMEM((8, 4 * EX, TILE), BF16),
            pltpu.VMEM((GROUP, 4 * EX, TILE), BF16),
            pltpu.VMEM((GROUP, EX, 256), F32),
            dma((4,)),
            dma((2 + EX,)),
            dma((EX, 4)),
            dma((EX, 4)),
            dma((EX, 4)),
            dma((EX, 4)),
            dma((EX, 4)),
            dma((EX, 4)),
            dma((4,)),
            dma((4,)),
            dma((2,)),
            dma((2,)),
        ],
        compiler_params=pltpu.CompilerParams(
            collective_id=0, has_side_effects=True, vmem_limit_bytes=56 * 1024 * 1024
        ),
        cost_estimate=pl.CostEstimate(flops=9_000_000_000, bytes_accessed=8_000_000, transcendentals=0),
    )(inputs, cotangents, jl_bank, *turned, test_features)


def solution(mesh):
    placed = (
        P("ex", None, "param"),
        P(None, "ex", None, "param"),
        P(),
        P(),
        P(),
        P(),
        P("ex", "param"),
    )
    return jax.shard_map(
        local, mesh=mesh, in_specs=placed, out_specs=P("ex", None), check_vma=False
    )
```

```python
import functools
import math

import jax
import jax.numpy as jnp
from jax import lax
from jax.experimental import pallas as pl
from jax.experimental.pallas import tpu as pltpu
from jax.sharding import PartitionSpec as P

D = 4096
K = 4096
TILE = 128
HITS = 8
MATS = 3
TOK = 128
BANK = 64
BLOCKS = 32
EX = 4
ROWS = 8
COLS = 4
PAIRS = MATS * COLS // 2
GROUP = 32
BATCH = 2
UNROLL = 64
MESH = pl.DeviceIdType.MESH
F32 = jnp.float32
BF16 = jnp.bfloat16
SCALE = 1.0 / (math.sqrt(TOK * MATS * HITS * D * D / (TILE * K)) * math.sqrt(K))
ORDER = (0, 2, 1, 3)


def dot(a, b):
    return lax.dot_general(a, b, (((1,), (0,)), ((), ())), preferred_element_type=F32)


def count_hits(hits, count, z, y, core):
    lane = lax.broadcasted_iota(jnp.int32, (HITS, TILE), 1)
    block_of_lane = lax.rem(lane, BLOCKS).astype(F32)
    quarter = lane // BLOCKS
    tile_of_row = lax.broadcasted_iota(jnp.int32, (BANK, 2 * TILE), 0).astype(F32)
    for kind in range(2):
        first, step = (z * 8 + core, 2) if kind == 0 else (y * 2 + core, 8)
        source = lax.broadcasted_iota(jnp.int32, (GROUP, COLS * TILE), 0)
        column = lax.broadcasted_iota(jnp.int32, (GROUP, COLS * TILE), 1) // TILE
        choose = jnp.where(source == first + step * column, 1.0, 0.0).astype(BF16)
        for m in range(MATS):
            spread = []
            for which in range(3):
                if kind == 0:
                    rows = [
                        hits[which, m, pl.ds(zz * 8 + y * 2, 2)].reshape(2 * HITS, GROUP)
                        for zz in range(4)
                    ]
                    values = jnp.concatenate(rows, axis=0)
                else:
                    values = hits[which, m, pl.ds(z * 8, ROWS)].reshape(ROWS * HITS, GROUP)
                spread.append(dot(values.astype(F32).astype(BF16), choose))

            def lanes_of(values, col, half):
                parts = [
                    values[(half * 4 + q) * HITS : (half * 4 + q + 1) * HITS, col * TILE : (col + 1) * TILE]
                    for q in range(4)
                ]
                low = jnp.where(quarter == 0, parts[0], parts[1])
                high = jnp.where(quarter == 2, parts[2], parts[3])
                return jnp.where(quarter < 2, low, high)

            for col in range(COLS):
                tile_rows, sign_rows = [], []
                for half in range(2):
                    tile, block, sign = [lanes_of(values, col, half) for values in spread]
                    tile_rows.append(jnp.where(block == block_of_lane, tile, -1.0))
                    sign_rows.append(2.0 * sign - 1.0)
                tile_rows = jnp.concatenate(tile_rows, axis=1)
                sign_rows = jnp.concatenate(sign_rows, axis=1)
                total = jnp.zeros((BANK, 2 * TILE), F32)
                for h in range(HITS):
                    total += jnp.where(
                        tile_of_row == tile_rows[h : h + 1, :], sign_rows[h : h + 1, :], 0.0
                    )
                at = (m * COLS + col) * BANK
                count[kind, at : at + BANK, :] = total.astype(BF16)


def turn_bank(bank, bank_t):
    def turn(r, carry):
        bank_t[pl.ds(r, TILE, stride=BANK), :] = bank[r].astype(F32).T
        return carry

    lax.fori_loop(0, BANK, turn, 0, unroll=32)


def turn_rows(ins, left32, left, e, slot):
    for i in range(ROWS):
        left32[slot, pl.ds(i, TILE, stride=ROWS), :] = ins[e, i].astype(F32).T
    left[slot] = left32[slot].astype(BF16)


def spread_bank(bank_t, weights):
    lower = lax.broadcasted_iota(jnp.int32, (TILE, 2 * BANK), 1) < BANK

    def step(a, carry):
        tiles = bank_t[pl.ds(pl.multiple_of(a * BANK, BANK), BANK), :]
        turned = jnp.concatenate([tiles, tiles], axis=0).T
        weights[a, 0:TILE] = jnp.where(lower, turned, 0.0).astype(BF16)
        weights[a, TILE:] = jnp.where(lower, 0.0, turned).astype(BF16)
        return carry

    lax.fori_loop(0, TILE, step, 0, unroll=32)


def gradient(left, cots, grads, e, slot):
    rows = left[slot]
    for m in range(MATS):
        halves = []
        for col in range(0, COLS, 2):
            right = jnp.concatenate([cots[e, col, m], cots[e, col + 1, m]], axis=1)
            halves.append(dot(rows, right).reshape(TILE, ROWS, 2 * TILE))
        at = (slot * MATS + m) * 2 * ROWS
        grads[:, at : at + 2 * ROWS, :] = jnp.concatenate(halves, axis=1).astype(BF16)


def project(grads, weights, quads):
    def step(two, carry):
        outs = [dot(grads[two * 2 + u], weights[two * 2 + u]) for u in range(2)]
        at = pl.multiple_of(two * 2 * ROWS, 2 * ROWS)
        for slot in range(BATCH):
            for pair in range(PAIRS):
                src = (slot * PAIRS + pair) * ROWS
                both = jnp.concatenate([out[src : src + ROWS] for out in outs], axis=0)
                quads[slot, pl.ds(at, 2 * ROWS), pair * TILE : (pair + 1) * TILE] = both.astype(BF16)
        return carry

    lax.fori_loop(0, TILE // 2, step, 0, unroll=UNROLL)


def select(quads, count, picked, slot, kind):
    row_in_group = lax.rem(lax.broadcasted_iota(jnp.int32, (TILE * ROWS, TILE), 0), ROWS)
    lane_group = lax.broadcasted_iota(jnp.int32, (TILE * ROWS, TILE), 1) // BLOCKS
    sums = dot(quads[slot], count[kind])
    folded = jnp.where(row_in_group >= 4, sums[:, TILE:], sums[:, :TILE])
    picked[slot] = jnp.where(lane_group == lax.rem(row_in_group, 4), folded, 0.0)
    total = picked[slot, pl.ds(0, TILE, stride=ROWS), :]
    for i in range(1, ROWS):
        total += picked[slot, pl.ds(i, TILE, stride=ROWS), :]
    turned = total.T
    return turned[0:32] + turned[32:64] + turned[64:96] + turned[96:128]


def kernel(
    in_hbm, cot_hbm, bank_hbm, tiles_hbm, blocks_hbm, signs_hbm, test_hbm, out_ref,
    bank, bank_t, weights, hits, cots, ins, left32, left, grads, quads, picked, count, tests, tests_t,
    raw, sums_out, sums_in, done,
    load_sem, own_sem, j_send, j_recv, i_send, i_recv, p_send, p_recv, t_send, t_recv, ex_send, ex_recv,
):
    me = lax.axis_index("param")
    mx = lax.axis_index("ex")
    core = lax.rem(me, 2)
    y = lax.rem(me // 2, 4)
    z = me // 8

    def device(zz, yy, cc):
        return (zz * 4 + yy) * 2 + cc

    def along_y(distance):
        return device(z, lax.rem(y + distance, 4), core)

    def along_z(distance):
        return device(lax.rem(z + distance, 4), y, core)

    sibling = device(z, y, 1 - core)
    family, member = me // 4, lax.rem(me, 4)
    alone = member == mx

    barrier = pltpu.get_barrier_semaphore()

    def greet(**to):
        pl.semaphore_signal(barrier, inc=1, device_id=to, device_id_type=MESH)

    for j in range(4):
        sender = family * 4 + j

        @pl.when(jnp.logical_or(sender != me, member != mx))
        def _(sender=sender):
            greet(param=sender, ex=member)

    for d in (2, 1, 3):
        greet(param=along_y(d))
        greet(param=along_z(d))
    greet(param=sibling)
    loads = [
        pltpu.make_async_copy(tiles_hbm, hits.at[0], load_sem.at[0]),
        pltpu.make_async_copy(blocks_hbm, hits.at[1], load_sem.at[1]),
        pltpu.make_async_copy(signs_hbm, hits.at[2], load_sem.at[2]),
        pltpu.make_async_copy(bank_hbm, bank, load_sem.at[3]),
    ]
    for copy in loads:
        copy.start()
    own = []
    for kind in range(2):
        pair = pl.ds(2 * kind, 2)
        col_pos, row_pos = (y, z) if kind == 0 else (z, y)
        own.append(
            pltpu.make_async_copy(
                in_hbm.at[pair], ins.at[pair, row_pos * 2 + core], own_sem.at[kind]
            )
        )
        for e in (2 * kind, 2 * kind + 1):
            own.append(
                pltpu.make_async_copy(cot_hbm.at[:, e], cots.at[e, col_pos], own_sem.at[2 + e])
            )
    for copy in own:
        copy.start()

    pl.semaphore_wait(barrier, 7 + jnp.where(alone, 3, 4))

    def send(src, dst, send_sem, recv_sem, **to):
        copy = pltpu.make_async_remote_copy(
            src_ref=src, dst_ref=dst, send_sem=send_sem, recv_sem=recv_sem, device_id=to, device_id_type=MESH
        )
        copy.start()
        return copy

    cols, rows, relays = {}, {}, {}
    early, late = ORDER[:BATCH], ORDER[BATCH:]

    def rings(e):
        return ((y, along_y), (z, along_z)) if e < 2 else ((z, along_z), (y, along_y))

    def send_tiles(batch):
        for e in batch:
            pos, to = rings(e)[1]
            place = ins.at[e, pos * 2 + core]
            for d in (2, 1, 3):
                rows[e, d] = send(in_hbm.at[e], place, i_send.at[e, d], i_recv.at[e, d], param=to(d))
            relays[e, 0] = send(in_hbm.at[e], place, p_send.at[e, 0], p_recv.at[e, 0], param=sibling)
        for e in batch:
            pos, to = rings(e)[0]
            for d in (2, 1, 3):
                cols[e, d] = send(
                    cot_hbm.at[:, e], cots.at[e, pos], j_send.at[e, d], j_recv.at[e, d], param=to(d)
                )

    def relay_rows(batch):
        for e in batch:
            pos = rings(e)[1][0]
            for d in (1, 3, 2):
                rows[e, d].wait_recv()
                place = ins.at[e, lax.rem(pos + 4 - d, 4) * 2 + core]
                relays[e, d] = send(place, place, p_send.at[e, d], p_recv.at[e, d], param=sibling)

    tests_out = []
    test_here = pltpu.make_async_copy(test_hbm, tests.at[member], t_recv.at[member])
    test_near = pltpu.make_async_remote_copy(
        src_ref=test_hbm,
        dst_ref=tests.at[member],
        send_sem=t_send.at[0],
        recv_sem=t_recv.at[member],
        device_id={"param": family * 4 + mx, "ex": mx},
        device_id_type=MESH,
    )

    def send_tests():
        for d in range(1, 4):
            tests_out.append(
                send(
                    test_hbm, tests.at[member], t_send.at[d], t_recv.at[member],
                    param=family * 4 + mx, ex=lax.rem(mx + d, 4),
                )
            )

        @pl.when(alone)
        def _():
            test_here.start()

        @pl.when(jnp.logical_not(alone))
        def _():
            test_near.start()

    def gradients(batch):
        for slot, e in enumerate(batch):
            for index in range(4):
                relays[e, index].wait_recv()
            turn_rows(ins, left32, left, e, slot)
        for slot, e in enumerate(batch):
            for d in (1, 3, 2):
                cols[e, d].wait_recv()
        if batch == late:
            send_tests()
        for slot, e in enumerate(batch):
            gradient(left, cots, grads, e, slot)

    def finish(batch):
        project(grads, weights, quads)
        for slot, e in enumerate(batch):
            raw[pl.ds(e, BLOCKS, stride=EX), :] = select(quads, count, picked, slot, e // 2)

    send_tiles(early)

    for copy in loads[:3]:
        copy.wait()
    count_hits(hits, count, z, y, core)
    loads[3].wait()
    turn_bank(bank, bank_t)
    for copy in own:
        copy.wait()
    relay_rows(early)
    send_tiles(late)
    spread_bank(bank_t, weights)
    gradients(early)
    relay_rows(late)
    finish(early)
    gradients(late)
    finish(late)
    sums_out[...] = raw[...].astype(BF16).reshape(8, 4 * EX, TILE)

    others = sorted(
        [(dz, dy, dc) for dz in range(4) for dy in range(4) for dc in range(2)][1:],
        key=lambda d: -(min(d[0], 4 - d[0]) + min(d[1], 4 - d[1])),
    )

    def exchange(index, source, incoming, beside=None):
        for dz, dy, dc in others:
            to = device(lax.rem(z + dz, 4), lax.rem(y + dy, 4), lax.rem(core + dc, 2))
            send(source(to), incoming.at[me], ex_send.at[index], ex_recv.at[index], param=to)
        if beside is not None:
            beside()
        rest = incoming.at[pl.ds(0, GROUP - 1)]
        pltpu.make_async_copy(rest, rest, ex_recv.at[index]).wait()
        return pltpu.make_async_copy(rest, rest, ex_send.at[index])

    def drain():
        for j in range(4):
            pltpu.make_async_copy(tests.at[j], tests.at[j], t_recv.at[j]).wait()
            for half in range(2):
                piece = tests[j, half * TILE : (half + 1) * TILE].astype(F32).T
                tests_t[j, :, half * TILE : (half + 1) * TILE] = piece.astype(BF16)
        for copy in [*cols.values(), *rows.values(), *relays.values(), *tests_out]:
            copy.wait_send()

        @pl.when(jnp.logical_not(alone))
        def _():
            test_near.wait_send()

    sums_in[me] = sums_out[family]
    sums_sent = exchange(0, lambda to: sums_out.at[to // 4], sums_in, drain)
    features = jnp.sum(sums_in[...].astype(F32), axis=0) * SCALE
    high = features.astype(BF16)
    low = (features - high.astype(F32)).astype(BF16)
    scores = jnp.zeros((2 * EX, 256), F32)
    for j in range(4):
        both = jnp.concatenate([high[j * EX : (j + 1) * EX], low[j * EX : (j + 1) * EX]], axis=0)
        scores += dot(both, tests_t[j])
    done[me] = scores[:EX] + scores[EX:]
    scores_sent = exchange(1, lambda to: done.at[me], done, sums_sent.wait)
    for j in range(4):
        total = done[j]
        for other in range(1, 8):
            total += done[other * 4 + j]
        out_ref[:, j * 256 : (j + 1) * 256] = total
    scores_sent.wait()


def local(inputs, cotangents, jl_bank, jl_tiles, jl_blocks, jl_signs, test_features):
    turned = [jnp.transpose(a, (0, 1, 3, 2)) for a in (jl_tiles, jl_blocks, jl_signs)]
    anywhere = pl.BlockSpec(memory_space=pl.ANY)
    dma = pltpu.SemaphoreType.DMA
    return pl.pallas_call(
        kernel,
        out_shape=jax.ShapeDtypeStruct((EX, 1024), F32),
        in_specs=[anywhere] * 7,
        out_specs=pl.BlockSpec(memory_space=pltpu.VMEM),
        scratch_shapes=[
            pltpu.VMEM((BANK, TILE, TILE), BF16),
            pltpu.VMEM((TILE * BANK, TILE), F32),
            pltpu.VMEM((TILE, 2 * TILE, 2 * BANK), BF16),
            pltpu.VMEM((3, MATS, GROUP, HITS, GROUP), jnp.int32),
            pltpu.VMEM((EX, COLS, MATS, TOK, TILE), BF16),
            pltpu.VMEM((EX, ROWS, TOK, TILE), BF16),
            pltpu.VMEM((BATCH, TILE * ROWS, TOK), F32),
            pltpu.VMEM((BATCH, TILE * ROWS, TOK), BF16),
            pltpu.VMEM((TILE, BATCH * PAIRS * ROWS, 2 * TILE), BF16),
            pltpu.VMEM((BATCH, TILE * ROWS, PAIRS * TILE), BF16),
            pltpu.VMEM((BATCH, TILE * ROWS, TILE), F32),
            pltpu.VMEM((2, MATS * COLS * BANK, 2 * TILE), BF16),
            pltpu.VMEM((4, 256, TILE), BF16),
            pltpu.VMEM((4, TILE, 256), BF16),
            pltpu.VMEM((BLOCKS * EX, TILE), F32),
            pltpu.VMEM((8, 4 * EX, TILE), BF16),
            pltpu.VMEM((GROUP, 4 * EX, TILE), BF16),
            pltpu.VMEM((GROUP, EX, 256), F32),
            dma((4,)),
            dma((2 + EX,)),
            dma((EX, 4)),
            dma((EX, 4)),
            dma((EX, 4)),
            dma((EX, 4)),
            dma((EX, 4)),
            dma((EX, 4)),
            dma((4,)),
            dma((4,)),
            dma((2,)),
            dma((2,)),
        ],
        compiler_params=pltpu.CompilerParams(
            collective_id=0, has_side_effects=True, vmem_limit_bytes=56 * 1024 * 1024
        ),
        cost_estimate=pl.CostEstimate(flops=9_000_000_000, bytes_accessed=8_000_000, transcendentals=0),
    )(inputs, cotangents, jl_bank, *turned, test_features)


def solution(mesh):
    placed = (
        P("ex", None, "param"),
        P(None, "ex", None, "param"),
        P(),
        P(),
        P(),
        P(),
        P("ex", "param"),
    )
    return jax.shard_map(
        local, mesh=mesh, in_specs=placed, out_specs=P("ex", None), check_vma=False
    )
```
